32 devices in a mesh: subj: 2 (over x), row: 8 (over z, y), col: 2 (over core).
Axes of the slice: x: 2, y: 2, z: 4, core: 2. Of those that a mesh axis runs over, the one named last changes fastest.
Arguments:
- series: float32 [256, 11392], P(('subj', 'row', 'col')), parts along dimension 0, may hold values from -30 to 30
- tap_values: float32 [17], replicated, may hold values from -4 to 4
- tap_count: int32 [1], replicated, may hold values from 4 to 8
- kept_frames: int32 [32], P('subj'), parts along dimension 0, may hold values from 1 to 8, 96 in all
- band_start: int32 [2], P('subj'), parts along dimension 0, may hold values from 0 to 7296
Outputs:
- fisher_band: bfloat16 [8192, 11392], P('subj', ('row', 'col')), parts along dimension 0
The draws below stay inside these ranges and needn't reach their ends.
There are 2 independent parts, one for each index of `subj`. The reference program is written for one: setup_inputs(seed, part) draws one part's arguments, and reference() takes and returns one part's arrays. A program takes and returns all parts, laid end to end along the dimension named above; an argument that names none is the same for every part. Nothing has to cross between parts.
Inputs may be any that keep to these rules, and one draw needn't show every extreme that they name: `tap_count`: frames farther than this from the centre get no weight. Time block d holds frames d * 8 to (d + 1) * 8 - 1; only its first kept_frames[d] frames are kept. `band_start`: the 4096 band grayordinates lie inside the grid.
All inputs are finite; a program needn't handle non-finite values.
Results may differ from the reference program's by a relative error of at most 0.0031.
The reference program's roundings to bfloat16 on the way (of `scaled`) count: a program that leaves them out, or rounds other values in their place, can miss the bound.
Values may be sent and summed in bfloat16 or wider, within the bound.
A program may use at most 128 MiB of HBM per device.

```python
import math
import jax
import jax.numpy as jnp
import numpy as np
from jax import lax

FR_DEV = 8
B = 4096
KMAX = 8
FRAMES = 128
G = 11392
N_ROW = 8
N_COL = 2


def draw_series(key, part):
    subkeys = jax.random.split(key, 4)
    network = jax.random.randint(subkeys[0], (G,), 0, 16)
    courses = jax.random.truncated_normal(subkeys[1], -4.0, 4.0, (FRAMES, 16), jnp.float32)
    loadings = jax.random.uniform(subkeys[2], (G,), jnp.float32, 0.5, 1.5)
    noise_part = jax.random.truncated_normal(subkeys[3], -4.0, 4.0, (FRAMES, G), jnp.float32)
    drift_scale = 3.0 - 2.0 * jnp.arange(FRAMES, dtype=jnp.float32) / FRAMES
    signal = jnp.take(courses, network, axis=1) * loadings
    return (signal + noise_part) * drift_scale[:, None]


def split_up(count, total, bound, slope):
    weights = [(1 << 20) // math.isqrt(rank ** slope) + 1 for rank in range(2, count + 1)]
    rest, holding = total - bound - (count - 1), [1] * (count - 1)
    while rest > 0:
        candidates = [i for i in range(count - 1) if holding[i] < bound]
        pool, budget = sum([weights[i] for i in candidates]), rest
        for i in candidates:
            extra = min(bound - holding[i], max(1, budget * weights[i] // pool), rest)
            holding[i] = holding[i] + extra
            rest = rest - extra
    return np.array([bound] + holding)


def uneven(stream_key, amount, total, limit, lean):
    if amount == 2:
        one = jax.random.randint(stream_key, (), max(1, total - limit), min(limit, total - 1) + 1)
        return jnp.stack([one, total - one])
    sizes = jnp.asarray(split_up(amount, total, limit, lean), jnp.int32)
    couples = (amount - 1) // 2
    giver, sink = sizes[1:1 + 2 * couples:2], sizes[2:2 + 2 * couples:2]
    slack = jnp.minimum(giver - 1, limit - sink)
    shifted = jax.random.randint(jax.random.fold_in(stream_key, 1), (couples,), 0, 1 << 20) % (slack + 1)
    sizes = sizes.at[1:1 + 2 * couples:2].set(giver - shifted).at[2:2 + 2 * couples:2].set(sink + shifted)
    return sizes[jax.random.permutation(jax.random.fold_in(stream_key, 2), amount)]


def bell_draw(rng, dims, deviation, bound, kind=jnp.bfloat16):
    values = deviation * jax.random.normal(rng, dims, jnp.float32)
    return jnp.clip(values, min=-bound, max=bound).astype(kind)


def setup_inputs(seed: int = 0, part: int = 0) -> dict:
    key_list = jax.random.split(jax.random.key(seed), 6)
    own_keys = jax.random.split(jax.random.fold_in(key_list[5], part), 6)
    return {
        "series": draw_series(jax.random.fold_in(jax.random.fold_in(key_list[5], part), 71), part),
        "tap_values": bell_draw(key_list[1], (2 * KMAX + 1,), 1.0, 4.0, jnp.float32),
        "tap_count": jax.random.randint(key_list[2], (1,), KMAX // 2, KMAX + 1).astype(jnp.int32),
        "kept_frames": uneven(own_keys[3], N_ROW * N_COL, 3 * FRAMES // 4, FR_DEV, 0).astype(jnp.int32),
        "band_start": jax.random.randint(own_keys[4], (1,), 0, G - B + 1).astype(jnp.int32),
    }


EPSILON = 1e-06
CLIP_LIMIT = 0.999

def tap_table(tap_values, tap_count):
    tap_reach = tap_values.shape[0] // 2
    offsets = jnp.arange(tap_values.shape[0], dtype=jnp.int32) - tap_reach
    active = (jnp.abs(offsets) <= tap_count[0]).astype(jnp.float32)
    centre = jnp.sum(active * tap_values) / jnp.sum(active)
    return active * (tap_values - centre)

def band_filter(padded, tap_weights, length):
    filtered = tap_weights[0] * padded[0:length]
    for tap_index in range(1, tap_weights.shape[0]):
        filtered = filtered + tap_weights[tap_index] * padded[tap_index:tap_index + length]
    return filtered

def keep_table(kept_frames, frames, block_len):
    positions = jnp.arange(frames, dtype=jnp.int32)
    return (positions % block_len < kept_frames[positions // block_len]).astype(jnp.float32)[:, None]

def normalize(filtered, keep_mask):
    centered = keep_mask * filtered
    spread = lax.optimization_barrier(jnp.sum(centered * centered, axis=0))
    return (centered * lax.rsqrt(spread + EPSILON)).astype(jnp.bfloat16)

def fisher_z(correlation):
    clipped = jnp.clip(correlation, -CLIP_LIMIT, CLIP_LIMIT)
    return 0.5 * (jnp.log1p(clipped) - jnp.log1p(-clipped))

def reference(series, tap_values, tap_count, kept_frames, band_start):
    tap_weights = tap_table(tap_values, tap_count)
    padded = jnp.pad(series, ((KMAX, KMAX), (0, 0)))
    filtered = band_filter(padded, tap_weights, FRAMES)
    keep_mask = keep_table(kept_frames, FRAMES, FR_DEV)
    scaled = normalize(filtered, keep_mask)
    band_cols = lax.dynamic_slice_in_dim(scaled, band_start[0], B, 1)
    correlation = lax.dot_general(band_cols, scaled, (((0,), (0,)), ((), ())), preferred_element_type=jnp.float32)
    return fisher_z(correlation).astype(jnp.bfloat16)
```

```python
import functools

import jax
import jax.numpy as jnp
from jax import lax
from jax.experimental import pallas as pl
from jax.experimental.pallas import tpu as pltpu
from jax.sharding import PartitionSpec as P

B = 4096
EPSILON = 1e-06
CLIP_LIMIT = 0.999
LANES = 128
TILE = 128
MESH = pl.DeviceIdType.MESH


def filter_rows(taps_ref, count_ref, kept_ref, tile, block, reach):
    shape = (TILE, TILE + 2 * reach)
    frame = lax.broadcasted_iota(jnp.int32, shape, 0)
    offset = lax.broadcasted_iota(jnp.int32, shape, 1) - frame
    taps = 2 * reach + 1
    total, amount = jnp.float32(0.0), jnp.float32(0.0)
    for j in range(taps):
        active = (count_ref[0] >= abs(j - reach)).astype(jnp.float32)
        total = total + active * taps_ref[j]
        amount = amount + active
    centre = jnp.full(shape, total) / jnp.full(shape, amount)
    rows = jnp.zeros(shape, jnp.float32)
    for j in range(taps):
        active = (count_ref[0] >= abs(j - reach)).astype(jnp.float32)
        rows = jnp.where(offset == j, active * (taps_ref[j] - centre), rows)
    kept = jnp.zeros(shape, jnp.int32)
    per = TILE // block
    for b in range(per):
        kept = jnp.where(frame // block == b, kept_ref[tile * per + b], kept)
    return jnp.where(frame % block < kept, rows, 0.0)


def band_kernel(start_ref, series_ref, own_ref):
    block, grays = series_ref.shape
    start = start_ref[0]
    base = jnp.minimum(start // LANES * LANES, grays - B - LANES)
    shift = start - base
    window = series_ref[:, pl.ds(pl.multiple_of(base, LANES), B + LANES)]
    lane = lax.broadcasted_iota(jnp.int32, (block, LANES), 1)
    back = (LANES - shift) % LANES
    turned = [
        pltpu.roll(window[:, k * LANES : (k + 1) * LANES], back, 1) for k in range(B // LANES + 1)
    ]
    for k in range(B // LANES):
        own_ref[:, k * LANES : (k + 1) * LANES] = jnp.where(
            lane < LANES - shift, turned[k], turned[k + 1]
        )


def exchange(sizes, series_ref, taps_ref, count_ref, kept_ref, own_ref, band_ref, cols_ref,
             band, cols, stage, held, band_send, band_recv, cols_send, cols_recv):
    n_row, n_col, low, width, reach = sizes
    n = n_row * n_col
    high = n_row // low
    block, grays = series_ref.shape
    frames = n * block
    wide = stage.shape[-1]
    subj, row, col = lax.axis_index("subj"), lax.axis_index("row"), lax.axis_index("col")
    me = row * n_col + col
    h, l = row // low, row % low

    def device(q):
        return (subj, q // n_col, q % n_col)

    barrier = pltpu.get_barrier_semaphore()

    def greet(k, carry):
        pl.semaphore_signal(barrier, inc=1, device_id=device((me + k) % n), device_id_type=MESH)
        return carry

    lax.fori_loop(1, n, greet, 0)

    band[me + 1] = own_ref[...]
    for p in range(n):
        first = p * width // LANES * LANES
        part = series_ref[:, first : min(first + wide + LANES, grays)]
        off = p * width - first
        if off:
            part = pltpu.roll(part, part.shape[1] - off, 1)
        stage[p] = part[:, :wide]
    cols[me + 1] = stage[me]
    for margin in (0, n + 1):
        band[margin] = jnp.zeros_like(band[margin])
        cols[margin] = jnp.zeros_like(cols[margin])

    pl.semaphore_wait(barrier, n - 1)

    started = []

    def band_copy(q, to, site):
        return pltpu.make_async_remote_copy(
            src_ref=band.at[q + 1], dst_ref=band.at[q + 1], send_sem=band_send.at[site],
            recv_sem=band_recv.at[q], device_id=device(to), device_id_type=MESH,
        )

    def send(q, to, ok):
        site = len(started)
        started.append((q, to, ok))

        @pl.when(ok)
        def _():
            band_copy(q, to, site).start()

    def arrived(q, ok):
        @pl.when(ok)
        def _():
            band_copy(q, (me + 1) % n, 0).wait_recv()

    def index(hh, ll, cc):
        return (hh * low + ll) * n_col + cc

    always = me >= 0

    def pass_on(q, ok, upward, downward):
        if upward:
            send(q, index(h + 1, l, col), ok & (h + 1 < high))
        if downward:
            send(q, index(h - 1, l, col), ok & (h > 0))
        for k in range(1, low):
            send(q, index(h, (l + k) % low, col), ok)
        share(q, ok)

    def share(q, ok):
        for k in range(1, n_col):
            send(q, index(h, l, (col + k) % n_col), ok)

    def across(hh, ok):
        for k in range(1, low):
            q = index(hh, (l + k) % low, col)
            arrived(q, ok)
            share(q, ok)

    def cols_copy(p, sender):
        return pltpu.make_async_remote_copy(
            src_ref=stage.at[p], dst_ref=cols.at[sender + 1], send_sem=cols_send.at[p],
            recv_sem=cols_recv.at[sender], device_id=device(p), device_id_type=MESH,
        )

    pass_on(me, always, True, True)

    def cols_start(k, carry):
        cols_copy((me + k) % n, me).start()
        return carry

    lax.fori_loop(1, n, cols_start, 0)

    for s in range(high):
        if s < high - 1:
            below, above = h - 1 - s, h + 1 + s
            q = index(below, l, col)
            arrived(q, below >= 0)
            pass_on(q, below >= 0, True, False)
            q = index(above, l, col)
            arrived(q, above < high)
            pass_on(q, above < high, False, True)
        if s == 0:
            across(h, always)
        else:
            across(h - s, h - s >= 0)
            across(h + s, h + s < high)

    def cols_wait(k, carry):
        other = (me + k) % n
        cols_copy(other, me).wait_send()
        cols_copy(other, other).wait_recv()
        return carry

    lax.fori_loop(1, n, cols_wait, 0)

    tiles = frames // TILE
    per = TILE // block
    chunk = held.shape[-1]

    def scaled(raw, at):
        spread = jnp.zeros((1, chunk), jnp.float32)
        for i in range(tiles):
            weights = filter_rows(taps_ref, count_ref, kept_ref, i, block, reach)
            x = raw[i * per : (i + 1) * per + 2, :, pl.ds(at, chunk)]
            masked = lax.dot_general(
                weights, x.reshape(TILE + 2 * reach, chunk), (((1,), (0,)), ((), ())),
                precision=lax.Precision.HIGHEST, preferred_element_type=jnp.float32,
            )
            spread = spread + jnp.sum(masked * masked, axis=0, keepdims=True)
            held[i * TILE : (i + 1) * TILE] = masked
        factor = lax.rsqrt(spread + EPSILON)
        return (held[...] * factor).astype(jnp.bfloat16)

    for at in range(0, wide, chunk):
        cols_ref[:, at : at + chunk] = scaled(cols, at)

    for hh in range(high):
        for ll in range(low):
            for k in range(1, n_col):
                arrived(index(hh, ll, (col + k) % n_col), always)

    def band_chunk(c, carry):
        at = pl.multiple_of(c * chunk, chunk)
        band_ref[:, pl.ds(at, chunk)] = scaled(band, at)
        return carry

    lax.fori_loop(0, B // chunk, band_chunk, 0)

    for site, (q, to, ok) in enumerate(started):
        @pl.when(ok)
        def _(site=site, q=q, to=to):
            band_copy(q, to, site).wait_send()


def fisher_kernel(cols_ref, band_ref, out_ref):
    c = lax.dot_general(
        cols_ref[...], band_ref[...], (((0,), (0,)), ((), ())), preferred_element_type=jnp.float32
    )[: out_ref.shape[0]]
    c = jnp.clip(c, -CLIP_LIMIT, CLIP_LIMIT)
    out_ref[...] = (0.5 * (jnp.log(1.0 + c) - jnp.log(1.0 - c))).astype(out_ref.dtype)


def body(series, tap_values, tap_count, kept_frames, band_start):
    n_row, n_col = lax.axis_size("row"), lax.axis_size("col")
    n = n_row * n_col
    low = max(k for k in range(1, n_row + 1) if n_row % k == 0 and k * k <= n_row)
    block, grays = series.shape
    width = grays // n
    wide = -(-width // 256) * 256
    reach = tap_values.shape[0] // 2
    frames = n * block
    high = n_row // low
    sites = (2 + low) + (high - 1) * 2 * (1 + low) + 2 * high * low
    smem = pl.BlockSpec(memory_space=pltpu.SMEM)
    vmem = pl.BlockSpec(memory_space=pltpu.VMEM)
    own = pl.pallas_call(
        band_kernel,
        out_shape=jax.ShapeDtypeStruct((block, B), series.dtype),
        in_specs=[smem, vmem],
        out_specs=vmem,
        compiler_params=pltpu.CompilerParams(vmem_limit_bytes=32 * 1024 * 1024),
    )(band_start, series)
    band, cols = pl.pallas_call(
        functools.partial(exchange, (n_row, n_col, low, width, reach)),
        out_shape=[
            jax.ShapeDtypeStruct((frames, B), jnp.bfloat16),
            jax.ShapeDtypeStruct((frames, wide), jnp.bfloat16),
        ],
        in_specs=[vmem, smem, smem, smem, vmem],
        out_specs=[vmem, vmem],
        scratch_shapes=[
            pltpu.VMEM((n + 2, block, B), jnp.float32),
            pltpu.VMEM((n + 2, block, wide), jnp.float32),
            pltpu.VMEM((n, block, wide), jnp.float32),
            pltpu.VMEM((frames, 256), jnp.float32),
            pltpu.SemaphoreType.DMA((sites,)),
            pltpu.SemaphoreType.DMA((n,)),
            pltpu.SemaphoreType.DMA((n,)),
            pltpu.SemaphoreType.DMA((n,)),
        ],
        compiler_params=pltpu.CompilerParams(
            collective_id=0, has_side_effects=True, vmem_limit_bytes=48 * 1024 * 1024
        ),
    )(series, tap_values, tap_count, kept_frames, own)
    step = 512
    out = pl.pallas_call(
        fisher_kernel,
        grid=(B // step,),
        out_shape=jax.ShapeDtypeStruct((width, B), jnp.bfloat16),
        in_specs=[
            pl.BlockSpec((frames, wide), lambda i: (0, 0)),
            pl.BlockSpec((frames, step), lambda i: (0, i)),
        ],
        out_specs=pl.BlockSpec((width, step), lambda i: (0, i)),
        compiler_params=pltpu.CompilerParams(vmem_limit_bytes=32 * 1024 * 1024),
    )(cols, band)
    return out.T


def solution(mesh):
    placed = (P(("subj", "row", "col"), None), P(), P(), P("subj"), P("subj"))
    return jax.shard_map(
        body, mesh=mesh, in_specs=placed, out_specs=P("subj", ("row", "col")), check_vma=False
    )
```

```python
import functools

import jax
import jax.numpy as jnp
from jax import lax
from jax.experimental import pallas as pl
from jax.experimental.pallas import tpu as pltpu
from jax.sharding import PartitionSpec as P

B = 4096
EPSILON = 1e-06
CLIP_LIMIT = 0.999
LANES = 128
TILE = 128
MESH = pl.DeviceIdType.MESH


def filter_rows(taps_ref, count_ref, kept_ref, tile, block, reach):
    shape = (TILE, TILE + 2 * reach)
    frame = lax.broadcasted_iota(jnp.int32, shape, 0)
    offset = lax.broadcasted_iota(jnp.int32, shape, 1) - frame
    taps = 2 * reach + 1
    total, amount = jnp.float32(0.0), jnp.float32(0.0)
    for j in range(taps):
        active = (count_ref[0] >= abs(j - reach)).astype(jnp.float32)
        total = total + active * taps_ref[j]
        amount = amount + active
    centre = jnp.full(shape, total) / jnp.full(shape, amount)
    rows = jnp.zeros(shape, jnp.float32)
    for j in range(taps):
        active = (count_ref[0] >= abs(j - reach)).astype(jnp.float32)
        rows = jnp.where(offset == j, active * (taps_ref[j] - centre), rows)
    kept = jnp.zeros(shape, jnp.int32)
    per = TILE // block
    for b in range(per):
        kept = jnp.where(frame // block == b, kept_ref[tile * per + b], kept)
    return jnp.where(frame % block < kept, rows, 0.0)


def prepare(sizes, series_hbm, taps_hbm, count_hbm, kept_hbm, start_hbm, own_ref, stage_ref,
            weights_ref, series_ref, taps_ref, count_ref, kept_ref, start_ref, sems):
    n, width, reach = sizes
    block, grays = series_ref.shape
    wide = stage_ref.shape[-1]
    pairs = (
        (taps_hbm, taps_ref), (count_hbm, count_ref), (kept_hbm, kept_ref),
        (start_hbm, start_ref), (series_hbm, series_ref),
    )
    copies = [pltpu.make_async_copy(a, b, sems.at[i]) for i, (a, b) in enumerate(pairs)]
    for copy in copies:
        copy.start()
    for copy in copies[:-1]:
        copy.wait()
    for i in range(weights_ref.shape[0]):
        weights_ref[i] = filter_rows(taps_ref, count_ref, kept_ref, i, block, reach)
    copies[-1].wait()
    start = start_ref[0]
    base = jnp.minimum(start // LANES * LANES, grays - B - LANES)
    shift = start - base
    window = series_ref[:, pl.ds(pl.multiple_of(base, LANES), B + LANES)]
    lane = lax.broadcasted_iota(jnp.int32, (block, LANES), 1)
    back = (LANES - shift) % LANES
    turned = [
        pltpu.roll(window[:, k * LANES : (k + 1) * LANES], back, 1) for k in range(B // LANES + 1)
    ]
    piece = own_ref.shape[-1]
    for k in range(B // LANES):
        at = k * LANES
        own_ref[at // piece, :, at % piece : at % piece + LANES] = jnp.where(
            lane < LANES - shift, turned[k], turned[k + 1]
        )
    for p in range(n):
        first = p * width // LANES * LANES
        part = series_ref[:, first : min(first + wide + LANES, grays)]
        off = p * width - first
        if off:
            part = pltpu.roll(part, part.shape[1] - off, 1)
        stage_ref[p] = part[:, :wide]


def exchange(sizes, own_ref, stage_ref, weights_ref, band_ref, cols_ref, raw, cols, held,
             own_send, own_recv, cols_send, cols_recv, band_send, band_recv):
    n_row, n_col, low = sizes
    n = n_row * n_col
    high = n_row // low
    pieces, block, piece = own_ref.shape
    frames = n * block
    wide = stage_ref.shape[-1]
    subj, row, col = lax.axis_index("subj"), lax.axis_index("row"), lax.axis_index("col")
    me = row * n_col + col
    h, l = row // low, row % low

    def device(q):
        return (subj, q // n_col, q % n_col)

    barrier = pltpu.get_barrier_semaphore()

    def greet(k, carry):
        pl.semaphore_signal(barrier, inc=1, device_id=device((me + k) % n), device_id_type=MESH)
        return carry

    lax.fori_loop(1, n, greet, 0)
    owner = me < pieces

    @pl.when(owner)
    def _():
        raw[me + 1] = own_ref[me % pieces]

    cols[me + 1] = stage_ref[me]
    for margin in (0, n + 1):
        raw[margin] = jnp.zeros_like(raw[margin])
        cols[margin] = jnp.zeros_like(cols[margin])
    pl.semaphore_wait(barrier, n - 1)

    def own_copy(p, sender):
        return pltpu.make_async_remote_copy(
            src_ref=own_ref.at[p], dst_ref=raw.at[sender + 1], send_sem=own_send.at[p],
            recv_sem=own_recv.at[sender], device_id=device(p), device_id_type=MESH,
        )

    def cols_copy(p, sender):
        return pltpu.make_async_remote_copy(
            src_ref=stage_ref.at[p], dst_ref=cols.at[sender + 1], send_sem=cols_send.at[p],
            recv_sem=cols_recv.at[sender], device_id=device(p), device_id_type=MESH,
        )

    def own_start(k, carry):
        p = (me + k) % n

        @pl.when(p < pieces)
        def _():
            own_copy(p, me).start()

        return carry

    lax.fori_loop(1, n, own_start, 0)

    def cols_start(k, carry):
        cols_copy((me + k) % n, me).start()
        return carry

    lax.fori_loop(1, n, cols_start, 0)

    tiles = frames // TILE
    per = TILE // block
    chunk = held.shape[-1]

    def scaled(source, at):
        spread = jnp.zeros((1, chunk), jnp.float32)
        for i in range(tiles):
            x = source[i * per : (i + 1) * per + 2, :, at : at + chunk]
            masked = lax.dot_general(
                weights_ref[i], x.reshape((per + 2) * block, chunk), (((1,), (0,)), ((), ())),
                precision=lax.Precision.HIGHEST, preferred_element_type=jnp.float32,
            )
            spread = spread + jnp.sum(masked * masked, axis=0, keepdims=True)
            if tiles > 1:
                held[i * TILE : (i + 1) * TILE] = masked
        if tiles > 1:
            masked = held[...]
        return (masked * lax.rsqrt(spread + EPSILON)).astype(jnp.bfloat16)

    @pl.when(owner)
    def _():
        def own_wait(k, carry):
            own_copy(0, (me + k) % n).wait_recv()
            return carry

        lax.fori_loop(1, n, own_wait, 0)
        for at in range(0, piece, chunk):
            band_ref[me % pieces, :, at : at + chunk] = scaled(raw, at)

    started = []

    def band_copy(q, to, site):
        return pltpu.make_async_remote_copy(
            src_ref=band_ref.at[q], dst_ref=band_ref.at[q], send_sem=band_send.at[site],
            recv_sem=band_recv.at[q], device_id=device(to), device_id_type=MESH,
        )

    def send(q, to, ok):
        site = len(started)
        started.append((q, to, ok))

        @pl.when(ok & (q < pieces))
        def _():
            band_copy(q, to, site).start()

    def arrived(q, ok):
        @pl.when(ok & (q < pieces))
        def _():
            band_copy(q, (me + 1) % n, 0).wait_recv()

    def index(hh, ll, cc):
        return (hh * low + ll) * n_col + cc

    always = me >= 0

    def share(q, ok):
        for k in range(1, n_col):
            send(q, index(h, l, (col + k) % n_col), ok)

    def pass_on(q, ok, upward, downward):
        if upward:
            send(q, index(h + 1, l, col), ok & (h + 1 < high))
        if downward:
            send(q, index(h - 1, l, col), ok & (h > 0))
        for k in range(1, low):
            send(q, index(h, (l + k) % low, col), ok)
        share(q, ok)

    def across(hh, ok):
        for k in range(1, low):
            q = index(hh, (l + k) % low, col)
            arrived(q, ok)
            share(q, ok)

    pass_on(me, always, True, True)
    for s in range(high):
        if s < high - 1:
            below, above = h - 1 - s, h + 1 + s
            q = index(below, l, col)
            arrived(q, below >= 0)
            pass_on(q, below >= 0, True, False)
            q = index(above, l, col)
            arrived(q, above < high)
            pass_on(q, above < high, False, True)
        if s == 0:
            across(h, always)
        else:
            across(h - s, h - s >= 0)
            across(h + s, h + s < high)

    def cols_wait(k, carry):
        cols_copy(0, (me + k) % n).wait_recv()
        return carry

    lax.fori_loop(1, n, cols_wait, 0)
    for at in range(0, wide, chunk):
        cols_ref[:, at : at + chunk] = scaled(cols, at)

    for hh in range(high):
        for ll in range(low):
            for k in range(1, n_col):
                arrived(index(hh, ll, (col + k) % n_col), always)

    def sent(k, carry):
        p = (me + k) % n
        cols_copy(p, me).wait_send()

        @pl.when(p < pieces)
        def _():
            own_copy(p, me).wait_send()

        return carry

    lax.fori_loop(1, n, sent, 0)
    for site, (q, to, ok) in enumerate(started):
        @pl.when(ok & (q < pieces))
        def _(site=site, q=q, to=to):
            band_copy(q, to, site).wait_send()


def fisher_kernel(cols_ref, band_ref, out_ref):
    c = lax.dot_general(
        cols_ref[...], band_ref[...], (((0,), (0,)), ((), ())), preferred_element_type=jnp.float32
    )[: out_ref.shape[0]]
    c = jnp.clip(c, -CLIP_LIMIT, CLIP_LIMIT)
    out_ref[...] = (0.5 * (jnp.log(1.0 + c) - jnp.log(1.0 - c))).astype(out_ref.dtype)


def body(series, tap_values, tap_count, kept_frames, band_start):
    n_row, n_col = lax.axis_size("row"), lax.axis_size("col")
    n = n_row * n_col
    low = max(k for k in range(1, n_row + 1) if n_row % k == 0 and k * k <= n_row)
    block, grays = series.shape
    width = grays // n
    wide = -(-width // 256) * 256
    reach = tap_values.shape[0] // 2
    frames = n * block
    high = n_row // low
    sites = (2 + low) + (high - 1) * 2 * (1 + low) + 2 * high * low
    pieces = min(n, B // LANES)
    piece = B // pieces
    chunk = min(piece, 256)
    tiles = frames // TILE
    anywhere = pl.BlockSpec(memory_space=pltpu.HBM)
    vmem = pl.BlockSpec(memory_space=pltpu.VMEM)
    f32, i32, bf16 = jnp.float32, jnp.int32, jnp.bfloat16
    own, stage, weights = pl.pallas_call(
        functools.partial(prepare, (n, width, reach)),
        out_shape=[
            jax.ShapeDtypeStruct((pieces, block, piece), f32),
            jax.ShapeDtypeStruct((n, block, wide), f32),
            jax.ShapeDtypeStruct((tiles, TILE, TILE + 2 * reach), f32),
        ],
        in_specs=[anywhere] * 5,
        out_specs=[vmem] * 3,
        scratch_shapes=[
            pltpu.VMEM(series.shape, f32),
            pltpu.SMEM(tap_values.shape, f32),
            pltpu.SMEM(tap_count.shape, i32),
            pltpu.SMEM(kept_frames.shape, i32),
            pltpu.SMEM(band_start.shape, i32),
            pltpu.SemaphoreType.DMA((5,)),
        ],
        compiler_params=pltpu.CompilerParams(vmem_limit_bytes=32 * 1024 * 1024),
    )(series, tap_values, tap_count, kept_frames, band_start)
    band, cols = pl.pallas_call(
        functools.partial(exchange, (n_row, n_col, low)),
        out_shape=[
            jax.ShapeDtypeStruct((pieces, frames, piece), bf16),
            jax.ShapeDtypeStruct((frames, wide), bf16),
        ],
        in_specs=[vmem] * 3,
        out_specs=[vmem] * 2,
        scratch_shapes=[
            pltpu.VMEM((n + 2, block, piece), f32),
            pltpu.VMEM((n + 2, block, wide), f32),
            pltpu.VMEM((frames, chunk), f32),
            pltpu.SemaphoreType.DMA((n,)),
            pltpu.SemaphoreType.DMA((n,)),
            pltpu.SemaphoreType.DMA((n,)),
            pltpu.SemaphoreType.DMA((n,)),
            pltpu.SemaphoreType.DMA((sites,)),
            pltpu.SemaphoreType.DMA((n,)),
        ],
        compiler_params=pltpu.CompilerParams(
            collective_id=0, has_side_effects=True, vmem_limit_bytes=40 * 1024 * 1024
        ),
    )(own, stage, weights)
    out = pl.pallas_call(
        fisher_kernel,
        grid=(pieces,),
        out_shape=jax.ShapeDtypeStruct((width, B), bf16),
        in_specs=[
            pl.BlockSpec((frames, wide), lambda i: (0, 0)),
            pl.BlockSpec((None, frames, piece), lambda i: (i, 0, 0)),
        ],
        out_specs=pl.BlockSpec((width, piece), lambda i: (0, i)),
        compiler_params=pltpu.CompilerParams(vmem_limit_bytes=32 * 1024 * 1024),
    )(cols, band)
    return out.T


def solution(mesh):
    placed = (P(("subj", "row", "col"), None), P(), P(), P("subj"), P("subj"))
    return jax.shard_map(
        body, mesh=mesh, in_specs=placed, out_specs=P("subj", ("row", "col")), check_vma=False
    )
```

```python
import functools

import jax
import jax.numpy as jnp
from jax import lax
from jax.experimental import pallas as pl
from jax.experimental.pallas import tpu as pltpu
from jax.sharding import PartitionSpec as P

B = 4096
EPSILON = 1e-06
CLIP_LIMIT = 0.999
LANES = 128
TILE = 128
MESH = pl.DeviceIdType.MESH


def filter_rows(taps_ref, count_ref, kept_ref, tile, block, reach):
    shape = (TILE, TILE + 2 * reach)
    frame = lax.broadcasted_iota(jnp.int32, shape, 0)
    offset = lax.broadcasted_iota(jnp.int32, shape, 1) - frame
    taps = 2 * reach + 1
    total, amount = jnp.float32(0.0), jnp.float32(0.0)
    for j in range(taps):
        active = (count_ref[0] >= abs(j - reach)).astype(jnp.float32)
        total = total + active * taps_ref[j]
        amount = amount + active
    centre = jnp.full(shape, total) / jnp.full(shape, amount)
    rows = jnp.zeros(shape, jnp.float32)
    for j in range(taps):
        active = (count_ref[0] >= abs(j - reach)).astype(jnp.float32)
        rows = jnp.where(offset == j, active * (taps_ref[j] - centre), rows)
    kept = jnp.zeros(shape, jnp.int32)
    per = TILE // block
    for b in range(per):
        kept = jnp.where(frame // block == b, kept_ref[tile * per + b], kept)
    return jnp.where(frame % block < kept, rows, 0.0)


def prepare(sizes, series_hbm, taps_hbm, count_hbm, kept_hbm, start_hbm, own_ref, stage_ref,
            weights_ref, series_ref, taps_ref, count_ref, kept_ref, start_ref, sems):
    n, width, reach = sizes
    block, grays = series_ref.shape
    wide = stage_ref.shape[-1]
    pairs = (
        (taps_hbm, taps_ref), (count_hbm, count_ref), (kept_hbm, kept_ref),
        (start_hbm, start_ref), (series_hbm, series_ref),
    )
    copies = [pltpu.make_async_copy(a, b, sems.at[i]) for i, (a, b) in enumerate(pairs)]
    for copy in copies:
        copy.start()
    for copy in copies[:-1]:
        copy.wait()
    for i in range(weights_ref.shape[0]):
        weights_ref[i] = filter_rows(taps_ref, count_ref, kept_ref, i, block, reach)
    copies[-1].wait()
    start = start_ref[0]
    base = jnp.minimum(start // LANES * LANES, grays - B - LANES)
    shift = start - base
    window = series_ref[:, pl.ds(pl.multiple_of(base, LANES), B + LANES)]
    lane = lax.broadcasted_iota(jnp.int32, (block, LANES), 1)
    back = (LANES - shift) % LANES
    turned = [
        pltpu.roll(window[:, k * LANES : (k + 1) * LANES], back, 1) for k in range(B // LANES + 1)
    ]
    piece = own_ref.shape[-1]
    for k in range(B // LANES):
        at = k * LANES
        own_ref[at // piece, :, at % piece : at % piece + LANES] = jnp.where(
            lane < LANES - shift, turned[k], turned[k + 1]
        )
    for p in range(n):
        first = p * width // LANES * LANES
        part = series_ref[:, first : min(first + wide + LANES, grays)]
        off = p * width - first
        if off:
            part = pltpu.roll(part, part.shape[1] - off, 1)
        stage_ref[p] = part[:, :wide]


def exchange(sizes, own_ref, stage_ref, weights_ref, out_ref, band_ref, turned, raw, cols, held,
             own_send, own_recv, cols_send, cols_recv, band_send, band_recv):
    n_row, n_col, low = sizes
    n = n_row * n_col
    high = n_row // low
    pieces, block, piece = own_ref.shape
    frames = n * block
    wide = stage_ref.shape[-1]
    subj, row, col = lax.axis_index("subj"), lax.axis_index("row"), lax.axis_index("col")
    me = row * n_col + col
    h, l = row // low, row % low

    def device(q):
        return (subj, q // n_col, q % n_col)

    barrier = pltpu.get_barrier_semaphore()

    def greet(k, carry):
        pl.semaphore_signal(barrier, inc=1, device_id=device((me + k) % n), device_id_type=MESH)
        return carry

    lax.fori_loop(1, n, greet, 0)
    owner = me < pieces

    @pl.when(owner)
    def _():
        raw[me + 1] = own_ref[me % pieces]

    cols[me + 1] = stage_ref[me]
    for margin in (0, n + 1):
        raw[margin] = jnp.zeros_like(raw[margin])
        cols[margin] = jnp.zeros_like(cols[margin])
    pl.semaphore_wait(barrier, n - 1)

    def own_copy(p, sender):
        return pltpu.make_async_remote_copy(
            src_ref=own_ref.at[p], dst_ref=raw.at[sender + 1], send_sem=own_send.at[p],
            recv_sem=own_recv.at[sender], device_id=device(p), device_id_type=MESH,
        )

    def cols_copy(p, sender):
        return pltpu.make_async_remote_copy(
            src_ref=stage_ref.at[p], dst_ref=cols.at[sender + 1], send_sem=cols_send.at[p],
            recv_sem=cols_recv.at[sender], device_id=device(p), device_id_type=MESH,
        )

    def own_start(k, carry):
        p = (me + k) % n

        @pl.when(p < pieces)
        def _():
            own_copy(p, me).start()

        return carry

    lax.fori_loop(1, n, own_start, 0)

    def cols_start(k, carry):
        cols_copy((me + k) % n, me).start()
        return carry

    lax.fori_loop(1, n, cols_start, 0)

    tiles = frames // TILE
    per = TILE // block
    chunk = held.shape[-1]

    def scaled(source, at):
        spread = jnp.zeros((1, chunk), jnp.float32)
        for i in range(tiles):
            x = source[i * per : (i + 1) * per + 2, :, at : at + chunk]
            masked = lax.dot_general(
                weights_ref[i], x.reshape((per + 2) * block, chunk), (((1,), (0,)), ((), ())),
                precision=lax.Precision.HIGHEST, preferred_element_type=jnp.float32,
            )
            spread = spread + jnp.sum(masked * masked, axis=0, keepdims=True)
            if tiles > 1:
                held[i * TILE : (i + 1) * TILE] = masked
        if tiles > 1:
            masked = held[...]
        return masked * lax.rsqrt(spread + EPSILON)

    @pl.when(owner)
    def _():
        def own_wait(k, carry):
            own_copy(0, (me + k) % n).wait_recv()
            return carry

        lax.fori_loop(1, n, own_wait, 0)
        for at in range(0, piece, chunk):
            band_ref[me % pieces, :, at : at + chunk] = scaled(raw, at).astype(jnp.bfloat16)

    started = []

    def band_copy(q, to, site):
        return pltpu.make_async_remote_copy(
            src_ref=band_ref.at[q], dst_ref=band_ref.at[q], send_sem=band_send.at[site],
            recv_sem=band_recv.at[q], device_id=device(to), device_id_type=MESH,
        )

    def send(what):
        site = len(started)
        started.append(what)
        q, to, ok = what()

        @pl.when(ok & (q < pieces))
        def _():
            band_copy(q, to, site).start()

    def arrived(q, ok):
        @pl.when(ok & (q < pieces))
        def _():
            band_copy(q, (me + 1) % n, 0).wait_recv()

    def index(hh, ll, cc):
        return (hh * low + ll) * n_col + cc

    def inside(hh):
        return (hh >= 0) & (hh < high)

    def share(hh, ll):
        for k in range(1, n_col):
            send(lambda k=k: (
                index(hh(), ll(), col), index(h, l, (col + k) % n_col), inside(hh())
            ))

    def pass_on(hh, upward, downward):
        if upward:
            send(lambda: (
                index(hh(), l, col), index(h + 1, l, col), inside(hh()) & (h + 1 < high)
            ))
        if downward:
            send(lambda: (index(hh(), l, col), index(h - 1, l, col), inside(hh()) & (h > 0)))
        for k in range(1, low):
            send(lambda k=k: (
                index(hh(), l, col), index(h, (l + k) % low, col), inside(hh())
            ))
        share(hh, lambda: l)

    def across(hh):
        for k in range(1, low):
            arrived(index(hh(), (l + k) % low, col), inside(hh()))
            share(hh, lambda k=k: (l + k) % low)

    def line(s):
        for hh, upward in ((lambda: h - 1 - s, True), (lambda: h + 1 + s, False)):
            arrived(index(hh(), l, col), inside(hh()))
            pass_on(hh, upward, not upward)

    def step(s):
        if s < high - 1:
            line(s)
        if s == 1:
            across(lambda: h)
        else:
            across(lambda: h - s + 1)
            across(lambda: h + s - 1)

    pass_on(lambda: h, True, True)
    if high > 1:
        line(0)

    def cols_wait(k, carry):
        cols_copy(0, (me + k) % n).wait_recv()
        return carry

    lax.fori_loop(1, n, cols_wait, 0)
    for at in range(0, wide, chunk):
        turned[at : at + chunk] = scaled(cols, at).T.astype(jnp.bfloat16)

    near = low * n_col
    rest = (high - 1) * low

    def fisher(i, carry):
        for s in range(1, high + 1):
            @pl.when(i == s)
            def _(s=s):
                step(s)

        j = jnp.maximum(i - near, 0)
        far = i >= near
        hh = jnp.where(far, (h + 1 + j % max(rest, 1) // low) % high, h)
        ll = jnp.where(far, j % low, (l + i // n_col) % low)
        cc = (col + jnp.where(far, j // max(rest, 1), i % n_col)) % n_col
        q = index(hh, ll, cc)
        arrived(q, cc != col)

        @pl.when(q < pieces)
        def _():
            c = lax.dot_general(
                turned[...], band_ref[q % pieces], (((1,), (0,)), ((), ())),
                preferred_element_type=jnp.float32,
            )[: out_ref.shape[0]]
            c = jnp.clip(c, -CLIP_LIMIT, CLIP_LIMIT)
            z = 0.5 * (jnp.log(1.0 + c) - jnp.log(1.0 - c))
            at = pl.multiple_of(q % pieces * piece, piece)
            out_ref[:, pl.ds(at, piece)] = z.astype(out_ref.dtype)

        return carry

    lax.fori_loop(0, n, fisher, 0)

    def sent(k, carry):
        p = (me + k) % n
        cols_copy(p, me).wait_send()

        @pl.when(p < pieces)
        def _():
            own_copy(p, me).wait_send()

        return carry

    lax.fori_loop(1, n, sent, 0)
    for site, what in enumerate(started):
        q, to, ok = what()

        @pl.when(ok & (q < pieces))
        def _(site=site, q=q, to=to):
            band_copy(q, to, site).wait_send()


def store(value_ref, out_hbm, sems):
    step = out_hbm.shape[1] // sems.shape[0]
    copies = []
    for i in range(sems.shape[0]):
        part = (slice(None), slice(i * step, (i + 1) * step))
        copies.append(pltpu.make_async_copy(value_ref.at[part], out_hbm.at[part], sems.at[i]))
        copies[-1].start()
    for copy in copies:
        copy.wait()


def body(series, tap_values, tap_count, kept_frames, band_start):
    n_row, n_col = lax.axis_size("row"), lax.axis_size("col")
    n = n_row * n_col
    low = max(k for k in range(1, n_row + 1) if n_row % k == 0 and k * k <= n_row)
    block, grays = series.shape
    width = grays // n
    wide = -(-width // 256) * 256
    reach = tap_values.shape[0] // 2
    frames = n * block
    high = n_row // low
    sites = (2 + low) + (high - 1) * 2 * (1 + low) + 2 * high * low
    pieces = min(n, B // LANES)
    piece = B // pieces
    chunk = min(piece, 256)
    tiles = frames // TILE
    anywhere = pl.BlockSpec(memory_space=pltpu.HBM)
    vmem = pl.BlockSpec(memory_space=pltpu.VMEM)
    f32, i32, bf16 = jnp.float32, jnp.int32, jnp.bfloat16
    own, stage, weights = pl.pallas_call(
        functools.partial(prepare, (n, width, reach)),
        out_shape=[
            jax.ShapeDtypeStruct((pieces, block, piece), f32),
            jax.ShapeDtypeStruct((n, block, wide), f32),
            jax.ShapeDtypeStruct((tiles, TILE, TILE + 2 * reach), f32),
        ],
        in_specs=[anywhere] * 5,
        out_specs=[vmem] * 3,
        scratch_shapes=[
            pltpu.VMEM(series.shape, f32),
            pltpu.SMEM(tap_values.shape, f32),
            pltpu.SMEM(tap_count.shape, i32),
            pltpu.SMEM(kept_frames.shape, i32),
            pltpu.SMEM(band_start.shape, i32),
            pltpu.SemaphoreType.DMA((5,)),
        ],
        compiler_params=pltpu.CompilerParams(vmem_limit_bytes=32 * 1024 * 1024),
    )(series, tap_values, tap_count, kept_frames, band_start)
    out = pl.pallas_call(
        functools.partial(exchange, (n_row, n_col, low)),
        out_shape=jax.ShapeDtypeStruct((width, B), bf16),
        in_specs=[vmem] * 3,
        out_specs=vmem,
        scratch_shapes=[
            pltpu.VMEM((pieces, frames, piece), bf16),
            pltpu.VMEM((wide, frames), bf16),
            pltpu.VMEM((n + 2, block, piece), f32),
            pltpu.VMEM((n + 2, block, wide), f32),
            pltpu.VMEM((frames, chunk), f32),
            pltpu.SemaphoreType.DMA((n,)),
            pltpu.SemaphoreType.DMA((n,)),
            pltpu.SemaphoreType.DMA((n,)),
            pltpu.SemaphoreType.DMA((n,)),
            pltpu.SemaphoreType.DMA((sites,)),
            pltpu.SemaphoreType.DMA((n,)),
        ],
        compiler_params=pltpu.CompilerParams(
            collective_id=0, has_side_effects=True, vmem_limit_bytes=40 * 1024 * 1024
        ),
    )(own, stage, weights)
    out = pl.pallas_call(
        store,
        out_shape=jax.ShapeDtypeStruct((width, B), bf16),
        in_specs=[vmem],
        out_specs=anywhere,
        scratch_shapes=[pltpu.SemaphoreType.DMA((4,))],
        compiler_params=pltpu.CompilerParams(vmem_limit_bytes=32 * 1024 * 1024),
    )(out)
    return out.T


def solution(mesh):
    placed = (P(("subj", "row", "col"), None), P(), P(), P("subj"), P("subj"))
    return jax.shard_map(
        body, mesh=mesh, in_specs=placed, out_specs=P("subj", ("row", "col")), check_vma=False
    )
```

```python
import functools

import jax
import jax.numpy as jnp
from jax import lax
from jax.experimental import pallas as pl
from jax.experimental.pallas import tpu as pltpu
from jax.sharding import PartitionSpec as P

B = 4096
EPSILON = 1e-06
CLIP_LIMIT = 0.999
LANES = 128
TILE = 128
MESH = pl.DeviceIdType.MESH


def filter_rows(taps_ref, count_ref, kept_ref, tile, block, reach):
    shape = (TILE, TILE + 2 * reach)
    frame = lax.broadcasted_iota(jnp.int32, shape, 0)
    offset = lax.broadcasted_iota(jnp.int32, shape, 1) - frame
    taps = 2 * reach + 1
    total, amount = jnp.float32(0.0), jnp.float32(0.0)
    for j in range(taps):
        active = (count_ref[0] >= abs(j - reach)).astype(jnp.float32)
        total = total + active * taps_ref[j]
        amount = amount + active
    centre = jnp.full(shape, total) / jnp.full(shape, amount)
    rows = jnp.zeros(shape, jnp.float32)
    for j in range(taps):
        active = (count_ref[0] >= abs(j - reach)).astype(jnp.float32)
        rows = jnp.where(offset == j, active * (taps_ref[j] - centre), rows)
    kept = jnp.zeros(shape, jnp.int32)
    per = TILE // block
    for b in range(per):
        kept = jnp.where(frame // block == b, kept_ref[tile * per + b], kept)
    return jnp.where(frame % block < kept, rows, 0.0)


def prepare(sizes, series_hbm, taps_hbm, count_hbm, kept_hbm, start_hbm, own_ref, stage_ref,
            weights_ref, series_ref, taps_ref, count_ref, kept_ref, start_ref, sems):
    n, width, reach = sizes
    block, grays = series_ref.shape
    subs, sub = stage_ref.shape[0], stage_ref.shape[-1]
    wide = subs * sub
    pairs = (
        (taps_hbm, taps_ref), (count_hbm, count_ref), (kept_hbm, kept_ref),
        (start_hbm, start_ref), (series_hbm, series_ref),
    )
    copies = [pltpu.make_async_copy(a, b, sems.at[i]) for i, (a, b) in enumerate(pairs)]
    for copy in copies:
        copy.start()
    for copy in copies[:-1]:
        copy.wait()
    for i in range(weights_ref.shape[0]):
        weights_ref[i] = filter_rows(taps_ref, count_ref, kept_ref, i, block, reach)
    copies[-1].wait()
    start = start_ref[0]
    base = jnp.minimum(start // LANES * LANES, grays - B - LANES)
    shift = start - base
    window = series_ref[:, pl.ds(pl.multiple_of(base, LANES), B + LANES)]
    lane = lax.broadcasted_iota(jnp.int32, (block, LANES), 1)
    back = (LANES - shift) % LANES
    turned = [
        pltpu.roll(window[:, k * LANES : (k + 1) * LANES], back, 1) for k in range(B // LANES + 1)
    ]
    piece = own_ref.shape[-1]
    for k in range(B // LANES):
        at = k * LANES
        own_ref[at // piece, :, at % piece : at % piece + LANES] = jnp.where(
            lane < LANES - shift, turned[k], turned[k + 1]
        )
    for p in range(n):
        first = p * width // LANES * LANES
        part = series_ref[:, first : min(first + wide + LANES, grays)]
        off = p * width - first
        if off:
            part = pltpu.roll(part, part.shape[1] - off, 1)
        for b in range(subs):
            stage_ref[b, p] = part[:, b * sub : (b + 1) * sub]


def exchange(sizes, own_ref, stage_ref, weights_ref, out_ref, band_ref, turned, raw, cols, held,
             own_send, own_recv, cols_send, cols_recv, band_send, band_recv):
    n_row, n_col, low = sizes
    n = n_row * n_col
    high = n_row // low
    pieces, block, piece = own_ref.shape
    frames = n * block
    subs, sub = stage_ref.shape[0], stage_ref.shape[-1]
    subj, row, col = lax.axis_index("subj"), lax.axis_index("row"), lax.axis_index("col")
    me = row * n_col + col
    h, l = row // low, row % low

    def device(q):
        return (subj, q // n_col, q % n_col)

    barrier = pltpu.get_barrier_semaphore()

    def greet(k, carry):
        pl.semaphore_signal(barrier, inc=1, device_id=device((me + k) % n), device_id_type=MESH)
        return carry

    lax.fori_loop(1, n, greet, 0)
    owner = me < pieces

    @pl.when(owner)
    def _():
        raw[me + 1] = own_ref[me % pieces]

    for b in range(subs):
        cols[b, me + 1] = stage_ref[b, me]
    for margin in (0, n + 1):
        raw[margin] = jnp.zeros_like(raw[margin])
        for b in range(subs):
            cols[b, margin] = jnp.zeros_like(cols[b, margin])
    pl.semaphore_wait(barrier, n - 1)

    def own_copy(p, sender):
        return pltpu.make_async_remote_copy(
            src_ref=own_ref.at[p], dst_ref=raw.at[sender + 1], send_sem=own_send.at[p],
            recv_sem=own_recv.at[sender], device_id=device(p), device_id_type=MESH,
        )

    def cols_copy(b, p, sender):
        return pltpu.make_async_remote_copy(
            src_ref=stage_ref.at[b, p], dst_ref=cols.at[b, sender + 1],
            send_sem=cols_send.at[b, p], recv_sem=cols_recv.at[b, sender], device_id=device(p), device_id_type=MESH,
        )

    def own_start(k, carry):
        p = (me + k) % n

        @pl.when(p < pieces)
        def _():
            own_copy(p, me).start()

        return carry

    lax.fori_loop(1, n, own_start, 0)

    for b in range(subs):
        def cols_start(k, carry, b=b):
            cols_copy(b, (me + k) % n, me).start()
            return carry

        lax.fori_loop(1, n, cols_start, 0)

    tiles = frames // TILE
    per = TILE // block
    chunk = min(piece, held.shape[-1])

    def scaled(load, chunk):
        spread = jnp.zeros((1, chunk), jnp.float32)
        for i in range(tiles):
            x = load(pl.ds(i * per, per + 2))
            masked = lax.dot_general(
                weights_ref[i], x.reshape((per + 2) * block, chunk), (((1,), (0,)), ((), ())),
                precision=lax.Precision.HIGHEST, preferred_element_type=jnp.float32,
            )
            spread = spread + jnp.sum(masked * masked, axis=0, keepdims=True)
            if tiles > 1:
                held[i * TILE : (i + 1) * TILE, :chunk] = masked
        if tiles > 1:
            masked = held[:, :chunk]
        return masked * lax.rsqrt(spread + EPSILON)

    @pl.when(owner)
    def _():
        def own_wait(k, carry):
            own_copy(0, (me + k) % n).wait_recv()
            return carry

        lax.fori_loop(1, n, own_wait, 0)
        for at in range(0, piece, chunk):
            band_ref[me % pieces, :, at : at + chunk] = scaled(
                lambda rows: raw[rows, :, at : at + chunk], chunk
            ).astype(jnp.bfloat16)

    started = []

    def band_copy(q, to, site):
        return pltpu.make_async_remote_copy(
            src_ref=band_ref.at[q], dst_ref=band_ref.at[q], send_sem=band_send.at[site],
            recv_sem=band_recv.at[q], device_id=device(to), device_id_type=MESH,
        )

    def send(what):
        site = len(started)
        started.append(what)
        q, to, ok = what()

        @pl.when(ok & (q < pieces))
        def _():
            band_copy(q, to, site).start()

    def arrived(q, ok):
        @pl.when(ok & (q < pieces))
        def _():
            band_copy(q, (me + 1) % n, 0).wait_recv()

    def index(hh, ll, cc):
        return (hh * low + ll) * n_col + cc

    def inside(hh):
        return (hh >= 0) & (hh < high)

    def share(hh, ll):
        for k in range(1, n_col):
            send(lambda k=k: (
                index(hh(), ll(), col), index(h, l, (col + k) % n_col), inside(hh())
            ))

    def pass_on(hh, upward, downward):
        if upward:
            send(lambda: (
                index(hh(), l, col), index(h + 1, l, col), inside(hh()) & (h + 1 < high)
            ))
        if downward:
            send(lambda: (index(hh(), l, col), index(h - 1, l, col), inside(hh()) & (h > 0)))
        for k in range(1, low):
            send(lambda k=k: (
                index(hh(), l, col), index(h, (l + k) % low, col), inside(hh())
            ))
        share(hh, lambda: l)

    def across(hh):
        for k in range(1, low):
            arrived(index(hh(), (l + k) % low, col), inside(hh()))
            share(hh, lambda k=k: (l + k) % low)

    def line(s):
        for hh, upward in ((lambda: h - 1 - s, True), (lambda: h + 1 + s, False)):
            arrived(index(hh(), l, col), inside(hh()))
            pass_on(hh, upward, not upward)

    def step(s):
        if s < high - 1:
            line(s)
        if s == 1:
            across(lambda: h)
        else:
            across(lambda: h - s + 1)
            across(lambda: h + s - 1)

    pass_on(lambda: h, True, True)
    if high > 1:
        line(0)

    def take_cols(b):
        def cols_wait(k, carry):
            cols_copy(b, 0, (me + k) % n).wait_recv()
            return carry

        lax.fori_loop(1, n, cols_wait, 0)
        turned[b] = scaled(lambda rows: cols[b, rows], sub).T.astype(jnp.bfloat16)

    def correlate(b, q):
        count = min(sub, out_ref.shape[0] - b * sub)
        c = lax.dot_general(
            turned[b], band_ref[q], (((1,), (0,)), ((), ())), preferred_element_type=jnp.float32
        )[:count]
        c = jnp.clip(c, -CLIP_LIMIT, CLIP_LIMIT)
        z = 0.5 * (jnp.log(1.0 + c) - jnp.log(1.0 - c))
        at = pl.multiple_of(q * piece, piece)
        out_ref[b * sub : b * sub + count, pl.ds(at, piece)] = z.astype(out_ref.dtype)

    take_cols(0)
    near = low * n_col
    rest = (high - 1) * low

    def fisher(i, carry):
        for s in range(1, high + 1):
            @pl.when(i == s)
            def _(s=s):
                step(s)

        j = jnp.maximum(i - near, 0)
        far = i >= near
        hh = jnp.where(far, (h + 1 + j % max(rest, 1) // low) % high, h)
        ll = jnp.where(far, j % low, (l + i // n_col) % low)
        cc = (col + jnp.where(far, j // max(rest, 1), i % n_col)) % n_col
        q = index(hh, ll, cc)
        arrived(q, cc != col)

        @pl.when(q < pieces)
        def _():
            correlate(0, q % pieces)

        return carry

    lax.fori_loop(0, n, fisher, 0)
    for b in range(1, subs):
        take_cols(b)

        def later(i, carry, b=b):
            for u in range(4):
                correlate(b, 4 * i + u)
            return carry

        lax.fori_loop(0, pieces // 4, later, 0)

    def sent(k, carry):
        p = (me + k) % n
        for b in range(subs):
            cols_copy(b, p, me).wait_send()

        @pl.when(p < pieces)
        def _():
            own_copy(p, me).wait_send()

        return carry

    lax.fori_loop(1, n, sent, 0)
    for site, what in enumerate(started):
        q, to, ok = what()

        @pl.when(ok & (q < pieces))
        def _(site=site, q=q, to=to):
            band_copy(q, to, site).wait_send()


def store(value_ref, out_hbm, sems):
    step = out_hbm.shape[1] // sems.shape[0]
    copies = []
    for i in range(sems.shape[0]):
        part = (slice(None), slice(i * step, (i + 1) * step))
        copies.append(pltpu.make_async_copy(value_ref.at[part], out_hbm.at[part], sems.at[i]))
        copies[-1].start()
    for copy in copies:
        copy.wait()


def body(series, tap_values, tap_count, kept_frames, band_start):
    n_row, n_col = lax.axis_size("row"), lax.axis_size("col")
    n = n_row * n_col
    low = max(k for k in range(1, n_row + 1) if n_row % k == 0 and k * k <= n_row)
    block, grays = series.shape
    width = grays // n
    sub = 256
    subs = -(-width // sub)
    reach = tap_values.shape[0] // 2
    frames = n * block
    high = n_row // low
    sites = (2 + low) + (high - 1) * 2 * (1 + low) + 2 * high * low
    pieces = min(n, B // LANES)
    piece = B // pieces
    tiles = frames // TILE
    anywhere = pl.BlockSpec(memory_space=pltpu.HBM)
    vmem = pl.BlockSpec(memory_space=pltpu.VMEM)
    f32, i32, bf16 = jnp.float32, jnp.int32, jnp.bfloat16
    own, stage, weights = pl.pallas_call(
        functools.partial(prepare, (n, width, reach)),
        out_shape=[
            jax.ShapeDtypeStruct((pieces, block, piece), f32),
            jax.ShapeDtypeStruct((subs, n, block, sub), f32),
            jax.ShapeDtypeStruct((tiles, TILE, TILE + 2 * reach), f32),
        ],
        in_specs=[anywhere] * 5,
        out_specs=[vmem] * 3,
        scratch_shapes=[
            pltpu.VMEM(series.shape, f32),
            pltpu.SMEM(tap_values.shape, f32),
            pltpu.SMEM(tap_count.shape, i32),
            pltpu.SMEM(kept_frames.shape, i32),
            pltpu.SMEM(band_start.shape, i32),
            pltpu.SemaphoreType.DMA((5,)),
        ],
        compiler_params=pltpu.CompilerParams(vmem_limit_bytes=32 * 1024 * 1024),
    )(series, tap_values, tap_count, kept_frames, band_start)
    out = pl.pallas_call(
        functools.partial(exchange, (n_row, n_col, low)),
        out_shape=jax.ShapeDtypeStruct((width, B), bf16),
        in_specs=[vmem] * 3,
        out_specs=vmem,
        scratch_shapes=[
            pltpu.VMEM((pieces, frames, piece), bf16),
            pltpu.VMEM((subs, sub, frames), bf16),
            pltpu.VMEM((n + 2, block, piece), f32),
            pltpu.VMEM((subs, n + 2, block, sub), f32),
            pltpu.VMEM((frames, sub), f32),
            pltpu.SemaphoreType.DMA((n,)),
            pltpu.SemaphoreType.DMA((n,)),
            pltpu.SemaphoreType.DMA((subs, n)),
            pltpu.SemaphoreType.DMA((subs, n)),
            pltpu.SemaphoreType.DMA((sites,)),
            pltpu.SemaphoreType.DMA((n,)),
        ],
        compiler_params=pltpu.CompilerParams(
            collective_id=0, has_side_effects=True, vmem_limit_bytes=40 * 1024 * 1024
        ),
    )(own, stage, weights)
    out = pl.pallas_call(
        store,
        out_shape=jax.ShapeDtypeStruct((width, B), bf16),
        in_specs=[vmem],
        out_specs=anywhere,
        scratch_shapes=[pltpu.SemaphoreType.DMA((4,))],
        compiler_params=pltpu.CompilerParams(vmem_limit_bytes=32 * 1024 * 1024),
    )(out)
    return out.T


def solution(mesh):
    placed = (P(("subj", "row", "col"), None), P(), P(), P("subj"), P("subj"))
    return jax.shard_map(
        body, mesh=mesh, in_specs=placed, out_specs=P("subj", ("row", "col")), check_vma=False
    )
```

```python
import functools

import jax
import jax.numpy as jnp
from jax import lax
from jax.experimental import pallas as pl
from jax.experimental.pallas import tpu as pltpu
from jax.sharding import PartitionSpec as P

B = 4096
EPSILON = 1e-06
CLIP_LIMIT = 0.999
LANES = 128
TILE = 128
MESH = pl.DeviceIdType.MESH


def filter_rows(taps_ref, count_ref, kept_ref, tile, block, reach):
    shape = (TILE, TILE + 2 * reach)
    frame = lax.broadcasted_iota(jnp.int32, shape, 0)
    offset = lax.broadcasted_iota(jnp.int32, shape, 1) - frame
    taps = 2 * reach + 1
    total, amount = jnp.float32(0.0), jnp.float32(0.0)
    for j in range(taps):
        active = (count_ref[0] >= abs(j - reach)).astype(jnp.float32)
        total = total + active * taps_ref[j]
        amount = amount + active
    centre = jnp.full(shape, total) / jnp.full(shape, amount)
    rows = jnp.zeros(shape, jnp.float32)
    for j in range(taps):
        active = (count_ref[0] >= abs(j - reach)).astype(jnp.float32)
        rows = jnp.where(offset == j, active * (taps_ref[j] - centre), rows)
    kept = jnp.zeros(shape, jnp.int32)
    per = TILE // block
    for b in range(per):
        kept = jnp.where(frame // block == b, kept_ref[tile * per + b], kept)
    return jnp.where(frame % block < kept, rows, 0.0)


def prepare(sizes, series_hbm, taps_hbm, count_hbm, kept_hbm, start_hbm, stage_ref,
            weights_ref, series_ref, taps_ref, count_ref, kept_ref, start_ref, sems):
    n, width, pieces, piece, reach = sizes
    block, grays = series_ref.shape
    plane = stage_ref.shape[0]
    wide = stage_ref.shape[-1] - piece
    pairs = (
        (taps_hbm, taps_ref), (count_hbm, count_ref), (kept_hbm, kept_ref),
        (start_hbm, start_ref), (series_hbm, series_ref),
    )
    copies = [pltpu.make_async_copy(a, b, sems.at[i]) for i, (a, b) in enumerate(pairs)]
    for copy in copies:
        copy.start()
    for copy in copies[:-1]:
        copy.wait()
    for i in range(weights_ref.shape[0]):
        weights_ref[i] = filter_rows(taps_ref, count_ref, kept_ref, i, block, reach)
    copies[-1].wait()
    start = start_ref[0]
    base = jnp.minimum(start // LANES * LANES, grays - B - LANES)
    shift = start - base
    window = series_ref[:, pl.ds(pl.multiple_of(base, LANES), B + LANES)]
    lane = lax.broadcasted_iota(jnp.int32, (block, LANES), 1)
    back = (LANES - shift) % LANES
    turned = [
        pltpu.roll(window[:, k * LANES : (k + 1) * LANES], back, 1) for k in range(B // LANES + 1)
    ]
    for k in range(B // LANES):
        at = k * LANES
        p, to = at // piece, wide + at % piece
        stage_ref[p % plane, p // plane, :, to : to + LANES] = jnp.where(
            lane < LANES - shift, turned[k], turned[k + 1]
        )
    for p in range(n):
        first = p * width // LANES * LANES
        part = series_ref[:, first : min(first + wide + LANES, grays)]
        off = p * width - first
        if off:
            part = pltpu.roll(part, part.shape[1] - off, 1)
        stage_ref[p % plane, p // plane, :, :wide] = part[:, :wide]
        if p >= pieces:
            stage_ref[p % plane, p // plane, :, wide:] = jnp.zeros((block, piece), part.dtype)


def exchange(sizes, stage_ref, weights_ref, out_ref, band_ref, turned, mid, raw, held,
             plane_send, plane_recv, line_send, line_recv, band_send, band_recv):
    n_row, n_col, low = sizes
    n = n_row * n_col
    high = n_row // low
    plane, _, block, _ = stage_ref.shape
    pieces, frames, piece = band_ref.shape
    wide = stage_ref.shape[-1] - piece
    subj, row, col = lax.axis_index("subj"), lax.axis_index("row"), lax.axis_index("col")
    me = row * n_col + col
    h, l = row // low, row % low
    own = l * n_col + col

    def device(q):
        return (subj, q // n_col, q % n_col)

    def beside(k):
        return (own + k) % plane

    def along(k):
        return (h + k) % high

    barrier = pltpu.get_barrier_semaphore()
    for k in range(1, plane):
        pl.semaphore_signal(
            barrier, inc=1, device_id=device(h * plane + beside(k)), device_id_type=MESH
        )
    for k in range(1, high):
        pl.semaphore_signal(
            barrier, inc=1, device_id=device(along(k) * plane + own), device_id_type=MESH
        )
    owner = me < pieces
    mid[own] = stage_ref[own]
    for margin in (0, n + 1):
        raw[margin] = jnp.zeros_like(raw[margin])
    pl.semaphore_wait(barrier, plane + high - 2)

    def plane_copy(to, sender):
        return pltpu.make_async_remote_copy(
            src_ref=stage_ref.at[to], dst_ref=mid.at[sender], send_sem=plane_send.at[to],
            recv_sem=plane_recv.at[sender], device_id=device(h * plane + to),
            device_id_type=MESH,
        )

    def line_copy(to, sender):
        return pltpu.make_async_remote_copy(
            src_ref=mid.at[:, to], dst_ref=raw.at[pl.ds(sender * plane + 1, plane)],
            send_sem=line_send.at[to], recv_sem=line_recv.at[sender],
            device_id=device(to * plane + own), device_id_type=MESH,
        )

    for k in range(1, plane):
        plane_copy(beside(k), own).start()
    for k in range(1, plane):
        plane_copy(beside(k), beside(k)).wait_recv()
    for k in range(1, high):
        line_copy(along(k), h).start()
    raw[pl.ds(h * plane + 1, plane)] = mid[:, h]

    tiles = frames // TILE
    per = TILE // block
    chunk = held.shape[-1]

    def scaled(at):
        spread = jnp.zeros((1, chunk), jnp.float32)
        for i in range(tiles):
            x = raw[i * per : (i + 1) * per + 2, :, at : at + chunk]
            masked = lax.dot_general(
                weights_ref[i], x.reshape((per + 2) * block, chunk), (((1,), (0,)), ((), ())),
                precision=lax.Precision.HIGHEST, preferred_element_type=jnp.float32,
            )
            spread = spread + jnp.sum(masked * masked, axis=0, keepdims=True)
            if tiles > 1:
                held[i * TILE : (i + 1) * TILE] = masked
        if tiles > 1:
            masked = held[...]
        return masked * lax.rsqrt(spread + EPSILON)

    for k in range(1, high):
        line_copy(along(k), along(k)).wait_recv()

    @pl.when(owner)
    def _():
        for at in range(0, piece, chunk):
            band_ref[me % pieces, :, at : at + chunk] = scaled(wide + at).astype(jnp.bfloat16)

    started = []

    def band_copy(q, to, site):
        return pltpu.make_async_remote_copy(
            src_ref=band_ref.at[q], dst_ref=band_ref.at[q], send_sem=band_send.at[site],
            recv_sem=band_recv.at[q], device_id=device(to), device_id_type=MESH,
        )

    def send(what):
        site = len(started)
        started.append(what)
        q, to, ok = what()

        @pl.when(ok & (q < pieces))
        def _():
            band_copy(q, to, site).start()

    def arrived(q, ok):
        @pl.when(ok & (q < pieces))
        def _():
            band_copy(q, (me + 1) % n, 0).wait_recv()

    def index(hh, ll, cc):
        return (hh * low + ll) * n_col + cc

    def inside(hh):
        return (hh >= 0) & (hh < high)

    def share(hh, ll):
        for k in range(1, n_col):
            send(lambda k=k: (
                index(hh(), ll(), col), index(h, l, (col + k) % n_col), inside(hh())
            ))

    def pass_on(hh, upward, downward):
        if upward:
            send(lambda: (
                index(hh(), l, col), index(h + 1, l, col), inside(hh()) & (h + 1 < high)
            ))
        if downward:
            send(lambda: (index(hh(), l, col), index(h - 1, l, col), inside(hh()) & (h > 0)))
        for k in range(1, low):
            send(lambda k=k: (
                index(hh(), l, col), index(h, (l + k) % low, col), inside(hh())
            ))
        share(hh, lambda: l)

    def across(hh):
        for k in range(1, low):
            arrived(index(hh(), (l + k) % low, col), inside(hh()))
            share(hh, lambda k=k: (l + k) % low)

    def line(s):
        for hh, upward in ((lambda: h - 1 - s, True), (lambda: h + 1 + s, False)):
            arrived(index(hh(), l, col), inside(hh()))
            pass_on(hh, upward, not upward)

    def step(s):
        if s < high - 1:
            line(s)
        if s == 1:
            across(lambda: h)
        else:
            across(lambda: h - s + 1)
            across(lambda: h + s - 1)

    pass_on(lambda: h, True, True)
    for at in range(0, wide, chunk):
        turned[at : at + chunk] = scaled(at).T.astype(jnp.bfloat16)
        if at == 0 and high > 1:
            line(0)

    near = low * n_col
    rest = (high - 1) * low

    def fisher(i, carry):
        for s in range(1, high + 1):
            @pl.when(i == s)
            def _(s=s):
                step(s)

        j = jnp.maximum(i - near, 0)
        far = i >= near
        hh = jnp.where(far, (h + 1 + j % max(rest, 1) // low) % high, h)
        ll = jnp.where(far, j % low, (l + i // n_col) % low)
        cc = (col + jnp.where(far, j // max(rest, 1), i % n_col)) % n_col
        q = index(hh, ll, cc)
        arrived(q, cc != col)

        @pl.when(q < pieces)
        def _():
            c = lax.dot_general(
                turned[...], band_ref[q % pieces], (((1,), (0,)), ((), ())),
                preferred_element_type=jnp.float32,
            )[: out_ref.shape[0]]
            c = jnp.clip(c, -CLIP_LIMIT, CLIP_LIMIT)
            z = 0.5 * (jnp.log(1.0 + c) - jnp.log(1.0 - c))
            at = pl.multiple_of(q % pieces * piece, piece)
            out_ref[:, pl.ds(at, piece)] = z.astype(out_ref.dtype)

        return carry

    lax.fori_loop(0, n, fisher, 0)

    for k in range(1, plane):
        plane_copy(beside(k), own).wait_send()
    for k in range(1, high):
        line_copy(along(k), h).wait_send()
    for site, what in enumerate(started):
        q, to, ok = what()

        @pl.when(ok & (q < pieces))
        def _(site=site, q=q, to=to):
            band_copy(q, to, site).wait_send()


def store(value_ref, out_hbm, sems):
    step = out_hbm.shape[1] // sems.shape[0]
    copies = []
    for i in range(sems.shape[0]):
        part = (slice(None), slice(i * step, (i + 1) * step))
        copies.append(pltpu.make_async_copy(value_ref.at[part], out_hbm.at[part], sems.at[i]))
        copies[-1].start()
    for copy in copies:
        copy.wait()


def body(series, tap_values, tap_count, kept_frames, band_start):
    n_row, n_col = lax.axis_size("row"), lax.axis_size("col")
    n = n_row * n_col
    low = max(k for k in range(1, n_row + 1) if n_row % k == 0 and k * k <= n_row)
    block, grays = series.shape
    width = grays // n
    wide = -(-width // 256) * 256
    reach = tap_values.shape[0] // 2
    frames = n * block
    high = n_row // low
    sites = (2 + low) + (high - 1) * 2 * (1 + low) + 2 * high * low
    pieces = min(n, B // LANES)
    piece = B // pieces
    chunk = min(piece, 256)
    tiles = frames // TILE
    anywhere = pl.BlockSpec(memory_space=pltpu.HBM)
    vmem = pl.BlockSpec(memory_space=pltpu.VMEM)
    f32, i32, bf16 = jnp.float32, jnp.int32, jnp.bfloat16
    plane = low * n_col
    stage, weights = pl.pallas_call(
        functools.partial(prepare, (n, width, pieces, piece, reach)),
        out_shape=[
            jax.ShapeDtypeStruct((plane, high, block, wide + piece), f32),
            jax.ShapeDtypeStruct((tiles, TILE, TILE + 2 * reach), f32),
        ],
        in_specs=[anywhere] * 5,
        out_specs=[vmem] * 2,
        scratch_shapes=[
            pltpu.VMEM(series.shape, f32),
            pltpu.SMEM(tap_values.shape, f32),
            pltpu.SMEM(tap_count.shape, i32),
            pltpu.SMEM(kept_frames.shape, i32),
            pltpu.SMEM(band_start.shape, i32),
            pltpu.SemaphoreType.DMA((5,)),
        ],
        compiler_params=pltpu.CompilerParams(vmem_limit_bytes=32 * 1024 * 1024),
    )(series, tap_values, tap_count, kept_frames, band_start)
    out = pl.pallas_call(
        functools.partial(exchange, (n_row, n_col, low)),
        out_shape=jax.ShapeDtypeStruct((width, B), bf16),
        in_specs=[vmem] * 2,
        out_specs=vmem,
        scratch_shapes=[
            pltpu.VMEM((pieces, frames, piece), bf16),
            pltpu.VMEM((wide, frames), bf16),
            pltpu.VMEM((plane, high, block, wide + piece), f32),
            pltpu.VMEM((n + 2, block, wide + piece), f32),
            pltpu.VMEM((frames, chunk), f32),
            pltpu.SemaphoreType.DMA((plane,)),
            pltpu.SemaphoreType.DMA((plane,)),
            pltpu.SemaphoreType.DMA((high,)),
            pltpu.SemaphoreType.DMA((high,)),
            pltpu.SemaphoreType.DMA((sites,)),
            pltpu.SemaphoreType.DMA((n,)),
        ],
        compiler_params=pltpu.CompilerParams(
            collective_id=0, has_side_effects=True, vmem_limit_bytes=40 * 1024 * 1024
        ),
    )(stage, weights)
    out = pl.pallas_call(
        store,
        out_shape=jax.ShapeDtypeStruct((width, B), bf16),
        in_specs=[vmem],
        out_specs=anywhere,
        scratch_shapes=[pltpu.SemaphoreType.DMA((4,))],
        compiler_params=pltpu.CompilerParams(vmem_limit_bytes=32 * 1024 * 1024),
    )(out)
    return out.T


def solution(mesh):
    placed = (P(("subj", "row", "col"), None), P(), P(), P("subj"), P("subj"))
    return jax.shard_map(
        body, mesh=mesh, in_specs=placed, out_specs=P("subj", ("row", "col")), check_vma=False
    )
```

```python
import functools

import jax
import jax.numpy as jnp
from jax import lax
from jax.experimental import pallas as pl
from jax.experimental.pallas import tpu as pltpu
from jax.sharding import PartitionSpec as P

B = 4096
EPSILON = 1e-06
CLIP_LIMIT = 0.999
LANES = 128
TILE = 128
MESH = pl.DeviceIdType.MESH


def filter_rows(taps_ref, count_ref, kept_ref, tile, block, reach):
    shape = (TILE, TILE + 2 * reach)
    frame = lax.broadcasted_iota(jnp.int32, shape, 0)
    offset = lax.broadcasted_iota(jnp.int32, shape, 1) - frame
    taps = 2 * reach + 1
    total, amount = jnp.float32(0.0), jnp.float32(0.0)
    for j in range(taps):
        active = (count_ref[0] >= abs(j - reach)).astype(jnp.float32)
        total = total + active * taps_ref[j]
        amount = amount + active
    centre = jnp.full(shape, total) / jnp.full(shape, amount)
    rows = jnp.zeros(shape, jnp.float32)
    for j in range(taps):
        active = (count_ref[0] >= abs(j - reach)).astype(jnp.float32)
        rows = jnp.where(offset == j, active * (taps_ref[j] - centre), rows)
    kept = jnp.zeros(shape, jnp.int32)
    per = TILE // block
    for b in range(per):
        kept = jnp.where(frame // block == b, kept_ref[tile * per + b], kept)
    return jnp.where(frame % block < kept, rows, 0.0)


def prepare(sizes, series_hbm, taps_hbm, count_hbm, kept_hbm, start_hbm, own_ref, stage_ref,
            weights_ref, series_ref, taps_ref, count_ref, kept_ref, start_ref, sems):
    n, width, reach = sizes
    block, grays = series_ref.shape
    wide = stage_ref.shape[-1]
    pairs = (
        (taps_hbm, taps_ref), (count_hbm, count_ref), (kept_hbm, kept_ref),
        (start_hbm, start_ref), (series_hbm, series_ref),
    )
    copies = [pltpu.make_async_copy(a, b, sems.at[i]) for i, (a, b) in enumerate(pairs)]
    for copy in copies:
        copy.start()
    for copy in copies[:-1]:
        copy.wait()
    for i in range(weights_ref.shape[0]):
        weights_ref[i] = filter_rows(taps_ref, count_ref, kept_ref, i, block, reach)
    copies[-1].wait()
    start = start_ref[0]
    base = jnp.minimum(start // LANES * LANES, grays - B - LANES)
    shift = start - base
    window = series_ref[:, pl.ds(pl.multiple_of(base, LANES), B + LANES)]
    lane = lax.broadcasted_iota(jnp.int32, (block, LANES), 1)
    back = (LANES - shift) % LANES
    turned = [
        pltpu.roll(window[:, k * LANES : (k + 1) * LANES], back, 1) for k in range(B // LANES + 1)
    ]
    piece = own_ref.shape[-1]
    for k in range(B // LANES):
        at = k * LANES
        own_ref[at // piece, :, at % piece : at % piece + LANES] = jnp.where(
            lane < LANES - shift, turned[k], turned[k + 1]
        )
    for p in range(n):
        first = p * width // LANES * LANES
        part = series_ref[:, first : min(first + wide + LANES, grays)]
        off = p * width - first
        if off:
            part = pltpu.roll(part, part.shape[1] - off, 1)
        stage_ref[p] = part[:, :wide]


def exchange(sizes, own_ref, stage_ref, weights_ref, band_ref, turned_ref, raw, cols, held,
             own_send, own_recv, cols_send, cols_recv, band_send, band_recv):
    n_row, n_col, low = sizes
    n = n_row * n_col
    high = n_row // low
    pieces, block, piece = own_ref.shape
    frames = n * block
    wide = stage_ref.shape[-1]
    subj, row, col = lax.axis_index("subj"), lax.axis_index("row"), lax.axis_index("col")
    me = row * n_col + col
    h, l = row // low, row % low

    def device(q):
        return (subj, q // n_col, q % n_col)

    barrier = pltpu.get_barrier_semaphore()

    def greet(k, carry):
        pl.semaphore_signal(barrier, inc=1, device_id=device((me + k) % n), device_id_type=MESH)
        return carry

    lax.fori_loop(1, n, greet, 0)
    owner = me < pieces

    @pl.when(owner)
    def _():
        raw[me + 1] = own_ref[me % pieces]

    cols[me + 1] = stage_ref[me]
    for margin in (0, n + 1):
        raw[margin] = jnp.zeros_like(raw[margin])
        cols[margin] = jnp.zeros_like(cols[margin])
    pl.semaphore_wait(barrier, n - 1)

    def own_copy(p, sender):
        return pltpu.make_async_remote_copy(
            src_ref=own_ref.at[p], dst_ref=raw.at[sender + 1], send_sem=own_send.at[p],
            recv_sem=own_recv.at[sender], device_id=device(p), device_id_type=MESH,
        )

    def cols_copy(p, sender):
        return pltpu.make_async_remote_copy(
            src_ref=stage_ref.at[p], dst_ref=cols.at[sender + 1], send_sem=cols_send.at[p],
            recv_sem=cols_recv.at[sender], device_id=device(p), device_id_type=MESH,
        )

    def own_start(k, carry):
        p = (me + k) % n

        @pl.when(p < pieces)
        def _():
            own_copy(p, me).start()

        return carry

    lax.fori_loop(1, n, own_start, 0)

    def cols_start(k, carry):
        cols_copy((me + k) % n, me).start()
        return carry

    lax.fori_loop(1, n, cols_start, 0)

    tiles = frames // TILE
    per = TILE // block
    chunk = held.shape[-1]

    def scaled(source, at):
        spread = jnp.zeros((1, chunk), jnp.float32)
        for i in range(tiles):
            x = source[i * per : (i + 1) * per + 2, :, at : at + chunk]
            masked = lax.dot_general(
                weights_ref[i], x.reshape((per + 2) * block, chunk), (((1,), (0,)), ((), ())),
                precision=lax.Precision.HIGHEST, preferred_element_type=jnp.float32,
            )
            spread = spread + jnp.sum(masked * masked, axis=0, keepdims=True)
            if tiles > 1:
                held[i * TILE : (i + 1) * TILE] = masked
        if tiles > 1:
            masked = held[...]
        return masked * lax.rsqrt(spread + EPSILON)

    @pl.when(owner)
    def _():
        def own_wait(k, carry):
            own_copy(0, (me + k) % n).wait_recv()
            return carry

        lax.fori_loop(1, n, own_wait, 0)
        for at in range(0, piece, chunk):
            band_ref[me % pieces, :, at : at + chunk] = scaled(raw, at).astype(jnp.bfloat16)

    started = []

    def band_copy(q, to, site):
        return pltpu.make_async_remote_copy(
            src_ref=band_ref.at[q], dst_ref=band_ref.at[q], send_sem=band_send.at[site],
            recv_sem=band_recv.at[q], device_id=device(to), device_id_type=MESH,
        )

    def send(q, to, ok):
        site = len(started)
        started.append((q, to, ok))

        @pl.when(ok & (q < pieces))
        def _():
            band_copy(q, to, site).start()

    def arrived(q, ok):
        @pl.when(ok & (q < pieces))
        def _():
            band_copy(q, (me + 1) % n, 0).wait_recv()

    def index(hh, ll, cc):
        return (hh * low + ll) * n_col + cc

    always = me >= 0

    def share(q, ok):
        for k in range(1, n_col):
            send(q, index(h, l, (col + k) % n_col), ok)

    def pass_on(q, ok, upward, downward):
        if upward:
            send(q, index(h + 1, l, col), ok & (h + 1 < high))
        if downward:
            send(q, index(h - 1, l, col), ok & (h > 0))
        for k in range(1, low):
            send(q, index(h, (l + k) % low, col), ok)
        share(q, ok)

    def across(hh, ok):
        for k in range(1, low):
            q = index(hh, (l + k) % low, col)
            arrived(q, ok)
            share(q, ok)

    pass_on(me, always, True, True)
    for s in range(high):
        if s < high - 1:
            below, above = h - 1 - s, h + 1 + s
            q = index(below, l, col)
            arrived(q, below >= 0)
            pass_on(q, below >= 0, True, False)
            q = index(above, l, col)
            arrived(q, above < high)
            pass_on(q, above < high, False, True)
        if s == 0:
            across(h, always)
        else:
            across(h - s, h - s >= 0)
            across(h + s, h + s < high)

    def cols_wait(k, carry):
        cols_copy(0, (me + k) % n).wait_recv()
        return carry

    lax.fori_loop(1, n, cols_wait, 0)
    for at in range(0, wide, chunk):
        turned_ref[at : at + chunk] = scaled(cols, at).T.astype(jnp.bfloat16)

    for hh in range(high):
        for ll in range(low):
            for k in range(1, n_col):
                arrived(index(hh, ll, (col + k) % n_col), always)

    def sent(k, carry):
        p = (me + k) % n
        cols_copy(p, me).wait_send()

        @pl.when(p < pieces)
        def _():
            own_copy(p, me).wait_send()

        return carry

    lax.fori_loop(1, n, sent, 0)
    for site, (q, to, ok) in enumerate(started):
        @pl.when(ok & (q < pieces))
        def _(site=site, q=q, to=to):
            band_copy(q, to, site).wait_send()


def fisher(turned_ref, band_ref, out_hbm, value, sems):
    pieces, _, piece = band_ref.shape

    def copy(q):
        part = (slice(None), pl.ds(pl.multiple_of(q * piece, piece), piece))
        return pltpu.make_async_copy(value.at[part], out_hbm.at[part], sems.at[q])

    def one(q, carry):
        c = lax.dot_general(
            turned_ref[...], band_ref[q], (((1,), (0,)), ((), ())),
            preferred_element_type=jnp.float32,
        )[: value.shape[0]]
        c = jnp.clip(c, -CLIP_LIMIT, CLIP_LIMIT)
        z = 0.5 * (jnp.log(1.0 + c) - jnp.log(1.0 - c))
        value[:, pl.ds(pl.multiple_of(q * piece, piece), piece)] = z.astype(value.dtype)
        copy(q).start()
        return carry

    def done(q, carry):
        copy(q).wait()
        return carry

    lax.fori_loop(0, pieces, one, 0)
    lax.fori_loop(0, pieces, done, 0)


def body(series, tap_values, tap_count, kept_frames, band_start):
    n_row, n_col = lax.axis_size("row"), lax.axis_size("col")
    n = n_row * n_col
    low = max(k for k in range(1, n_row + 1) if n_row % k == 0 and k * k <= n_row)
    block, grays = series.shape
    width = grays // n
    wide = -(-width // 256) * 256
    reach = tap_values.shape[0] // 2
    frames = n * block
    high = n_row // low
    sites = (2 + low) + (high - 1) * 2 * (1 + low) + 2 * high * low
    pieces = min(n, B // LANES)
    piece = B // pieces
    chunk = min(piece, 256)
    tiles = frames // TILE
    anywhere = pl.BlockSpec(memory_space=pltpu.HBM)
    vmem = pl.BlockSpec(memory_space=pltpu.VMEM)
    f32, i32, bf16 = jnp.float32, jnp.int32, jnp.bfloat16
    own, stage, weights = pl.pallas_call(
        functools.partial(prepare, (n, width, reach)),
        out_shape=[
            jax.ShapeDtypeStruct((pieces, block, piece), f32),
            jax.ShapeDtypeStruct((n, block, wide), f32),
            jax.ShapeDtypeStruct((tiles, TILE, TILE + 2 * reach), f32),
        ],
        in_specs=[anywhere] * 5,
        out_specs=[vmem] * 3,
        scratch_shapes=[
            pltpu.VMEM(series.shape, f32),
            pltpu.SMEM(tap_values.shape, f32),
            pltpu.SMEM(tap_count.shape, i32),
            pltpu.SMEM(kept_frames.shape, i32),
            pltpu.SMEM(band_start.shape, i32),
            pltpu.SemaphoreType.DMA((5,)),
        ],
        compiler_params=pltpu.CompilerParams(vmem_limit_bytes=32 * 1024 * 1024),
    )(series, tap_values, tap_count, kept_frames, band_start)
    band, turned = pl.pallas_call(
        functools.partial(exchange, (n_row, n_col, low)),
        out_shape=[
            jax.ShapeDtypeStruct((pieces, frames, piece), bf16),
            jax.ShapeDtypeStruct((wide, frames), bf16),
        ],
        in_specs=[vmem] * 3,
        out_specs=[vmem] * 2,
        scratch_shapes=[
            pltpu.VMEM((n + 2, block, piece), f32),
            pltpu.VMEM((n + 2, block, wide), f32),
            pltpu.VMEM((frames, chunk), f32),
            pltpu.SemaphoreType.DMA((n,)),
            pltpu.SemaphoreType.DMA((n,)),
            pltpu.SemaphoreType.DMA((n,)),
            pltpu.SemaphoreType.DMA((n,)),
            pltpu.SemaphoreType.DMA((sites,)),
            pltpu.SemaphoreType.DMA((n,)),
        ],
        compiler_params=pltpu.CompilerParams(
            collective_id=0, has_side_effects=True, vmem_limit_bytes=40 * 1024 * 1024
        ),
    )(own, stage, weights)
    out = pl.pallas_call(
        fisher,
        out_shape=jax.ShapeDtypeStruct((width, B), bf16),
        in_specs=[vmem] * 2,
        out_specs=anywhere,
        scratch_shapes=[
            pltpu.VMEM((width, B), bf16),
            pltpu.SemaphoreType.DMA((pieces,)),
        ],
        compiler_params=pltpu.CompilerParams(vmem_limit_bytes=32 * 1024 * 1024),
    )(turned, band)
    return out.T


def solution(mesh):
    placed = (P(("subj", "row", "col"), None), P(), P(), P("subj"), P("subj"))
    return jax.shard_map(
        body, mesh=mesh, in_specs=placed, out_specs=P("subj", ("row", "col")), check_vma=False
    )
```

```python
import functools

import jax
import jax.numpy as jnp
from jax import lax
from jax.experimental import pallas as pl
from jax.experimental.pallas import tpu as pltpu
from jax.sharding import PartitionSpec as P

B = 4096
EPSILON = 1e-06
CLIP_LIMIT = 0.999
LANES = 128
TILE = 128
MESH = pl.DeviceIdType.MESH


def filter_rows(taps_ref, count_ref, kept_ref, tile, block, reach):
    shape = (TILE, TILE + 2 * reach)
    frame = lax.broadcasted_iota(jnp.int32, shape, 0)
    offset = lax.broadcasted_iota(jnp.int32, shape, 1) - frame
    taps = 2 * reach + 1
    total, amount = jnp.float32(0.0), jnp.float32(0.0)
    for j in range(taps):
        active = (count_ref[0] >= abs(j - reach)).astype(jnp.float32)
        total = total + active * taps_ref[j]
        amount = amount + active
    centre = jnp.full(shape, total) / jnp.full(shape, amount)
    rows = jnp.zeros(shape, jnp.float32)
    for j in range(taps):
        active = (count_ref[0] >= abs(j - reach)).astype(jnp.float32)
        rows = jnp.where(offset == j, active * (taps_ref[j] - centre), rows)
    kept = jnp.zeros(shape, jnp.int32)
    per = TILE // block
    for b in range(per):
        kept = jnp.where(frame // block == b, kept_ref[tile * per + b], kept)
    return jnp.where(frame % block < kept, rows, 0.0)


def prepare(sizes, series_hbm, taps_hbm, count_hbm, kept_hbm, start_hbm, own_ref, stage_ref,
            weights_ref, series_ref, taps_ref, count_ref, kept_ref, start_ref, sems):
    n, width, reach = sizes
    block, grays = series_ref.shape
    wide = stage_ref.shape[-1]
    pairs = (
        (taps_hbm, taps_ref), (count_hbm, count_ref), (kept_hbm, kept_ref),
        (start_hbm, start_ref), (series_hbm, series_ref),
    )
    copies = [pltpu.make_async_copy(a, b, sems.at[i]) for i, (a, b) in enumerate(pairs)]
    for copy in copies:
        copy.start()
    for copy in copies[:-1]:
        copy.wait()
    for i in range(weights_ref.shape[0]):
        weights_ref[i] = filter_rows(taps_ref, count_ref, kept_ref, i, block, reach)
    copies[-1].wait()
    start = start_ref[0]
    base = jnp.minimum(start // LANES * LANES, grays - B - LANES)
    shift = start - base
    window = series_ref[:, pl.ds(pl.multiple_of(base, LANES), B + LANES)]
    lane = lax.broadcasted_iota(jnp.int32, (block, LANES), 1)
    back = (LANES - shift) % LANES
    turned = [
        pltpu.roll(window[:, k * LANES : (k + 1) * LANES], back, 1) for k in range(B // LANES + 1)
    ]
    piece = own_ref.shape[-1]
    for k in range(B // LANES):
        at = k * LANES
        own_ref[at // piece, :, at % piece : at % piece + LANES] = jnp.where(
            lane < LANES - shift, turned[k], turned[k + 1]
        )
    for p in range(n):
        first = p * width // LANES * LANES
        part = series_ref[:, first : min(first + wide + LANES, grays)]
        off = p * width - first
        if off:
            part = pltpu.roll(part, part.shape[1] - off, 1)
        stage_ref[p] = part[:, :wide]


def exchange(sizes, own_ref, stage_ref, weights_ref, band_ref, turned_ref, raw, cols, held,
             own_send, own_recv, cols_send, cols_recv, band_send, band_recv):
    n_row, n_col, low = sizes
    n = n_row * n_col
    high = n_row // low
    pieces, block, piece = own_ref.shape
    frames = n * block
    wide = stage_ref.shape[-1]
    subj, row, col = lax.axis_index("subj"), lax.axis_index("row"), lax.axis_index("col")
    me = row * n_col + col
    h, l = row // low, row % low

    def device(q):
        return (subj, q // n_col, q % n_col)

    barrier = pltpu.get_barrier_semaphore()

    def greet(k, carry):
        pl.semaphore_signal(barrier, inc=1, device_id=device((me + k) % n), device_id_type=MESH)
        return carry

    lax.fori_loop(1, n, greet, 0)
    owner = me < pieces

    @pl.when(owner)
    def _():
        raw[me + 1] = own_ref[me % pieces]

    cols[me + 1] = stage_ref[me]
    for margin in (0, n + 1):
        raw[margin] = jnp.zeros_like(raw[margin])
        cols[margin] = jnp.zeros_like(cols[margin])
    pl.semaphore_wait(barrier, n - 1)

    def own_copy(p, sender):
        return pltpu.make_async_remote_copy(
            src_ref=own_ref.at[p], dst_ref=raw.at[sender + 1], send_sem=own_send.at[p],
            recv_sem=own_recv.at[sender], device_id=device(p), device_id_type=MESH,
        )

    def cols_copy(p, sender):
        return pltpu.make_async_remote_copy(
            src_ref=stage_ref.at[p], dst_ref=cols.at[sender + 1], send_sem=cols_send.at[p],
            recv_sem=cols_recv.at[sender], device_id=device(p), device_id_type=MESH,
        )

    def own_start(k, carry):
        p = (me + k) % n

        @pl.when(p < pieces)
        def _():
            own_copy(p, me).start()

        return carry

    lax.fori_loop(1, n, own_start, 0)

    def cols_start(k, carry):
        cols_copy((me + k) % n, me).start()
        return carry

    lax.fori_loop(1, n, cols_start, 0)

    tiles = frames // TILE
    per = TILE // block
    chunk = held.shape[-1]

    def scaled(source, at):
        spread = jnp.zeros((1, chunk), jnp.float32)
        for i in range(tiles):
            x = source[i * per : (i + 1) * per + 2, :, at : at + chunk]
            masked = lax.dot_general(
                weights_ref[i], x.reshape((per + 2) * block, chunk), (((1,), (0,)), ((), ())),
                precision=lax.Precision.HIGHEST, preferred_element_type=jnp.float32,
            )
            spread = spread + jnp.sum(masked * masked, axis=0, keepdims=True)
            if tiles > 1:
                held[i * TILE : (i + 1) * TILE] = masked
        if tiles > 1:
            masked = held[...]
        return masked * lax.rsqrt(spread + EPSILON)

    @pl.when(owner)
    def _():
        def own_wait(k, carry):
            own_copy(0, (me + k) % n).wait_recv()
            return carry

        lax.fori_loop(1, n, own_wait, 0)
        for at in range(0, piece, chunk):
            band_ref[me % pieces, :, at : at + chunk] = scaled(raw, at).astype(jnp.bfloat16)

    started = []

    def band_copy(q, to, site):
        return pltpu.make_async_remote_copy(
            src_ref=band_ref.at[q], dst_ref=band_ref.at[q], send_sem=band_send.at[site],
            recv_sem=band_recv.at[q], device_id=device(to), device_id_type=MESH,
        )

    def send(q, to, ok):
        site = len(started)
        started.append((q, to, ok))

        @pl.when(ok & (q < pieces))
        def _():
            band_copy(q, to, site).start()

    def arrived(q, ok):
        @pl.when(ok & (q < pieces))
        def _():
            band_copy(q, (me + 1) % n, 0).wait_recv()

    def index(hh, ll, cc):
        return (hh * low + ll) * n_col + cc

    always = me >= 0

    def share(q, ok):
        for k in range(1, n_col):
            send(q, index(h, l, (col + k) % n_col), ok)

    def pass_on(q, ok, upward, downward):
        if upward:
            send(q, index(h + 1, l, col), ok & (h + 1 < high))
        if downward:
            send(q, index(h - 1, l, col), ok & (h > 0))
        for k in range(1, low):
            send(q, index(h, (l + k) % low, col), ok)
        share(q, ok)

    def across(hh, ok):
        for k in range(1, low):
            q = index(hh, (l + k) % low, col)
            arrived(q, ok)
            share(q, ok)

    pass_on(me, always, True, True)
    for s in range(high):
        if s < high - 1:
            below, above = h - 1 - s, h + 1 + s
            q = index(below, l, col)
            arrived(q, below >= 0)
            pass_on(q, below >= 0, True, False)
            q = index(above, l, col)
            arrived(q, above < high)
            pass_on(q, above < high, False, True)
        if s == 0:
            across(h, always)
        else:
            across(h - s, h - s >= 0)
            across(h + s, h + s < high)

    def cols_wait(k, carry):
        cols_copy(0, (me + k) % n).wait_recv()
        return carry

    lax.fori_loop(1, n, cols_wait, 0)
    for at in range(0, wide, chunk):
        turned_ref[at : at + chunk] = scaled(cols, at).T.astype(jnp.bfloat16)

    for hh in range(high):
        for ll in range(low):
            for k in range(1, n_col):
                arrived(index(hh, ll, (col + k) % n_col), always)

    def sent(k, carry):
        p = (me + k) % n
        cols_copy(p, me).wait_send()

        @pl.when(p < pieces)
        def _():
            own_copy(p, me).wait_send()

        return carry

    lax.fori_loop(1, n, sent, 0)
    for site, (q, to, ok) in enumerate(started):
        @pl.when(ok & (q < pieces))
        def _(site=site, q=q, to=to):
            band_copy(q, to, site).wait_send()


def fisher(turned_ref, band_ref, out_hbm, value, sems):
    pieces, _, piece = band_ref.shape

    def copy(q):
        part = (slice(None), pl.ds(pl.multiple_of(q * piece, piece), piece))
        return pltpu.make_async_copy(value.at[part], out_hbm.at[part], sems.at[q])

    def one(q, carry):
        c = lax.dot_general(
            turned_ref[...], band_ref[q], (((1,), (0,)), ((), ())),
            preferred_element_type=jnp.float32,
        )[: value.shape[0]]
        c = jnp.clip(c, -CLIP_LIMIT, CLIP_LIMIT)
        z = 0.5 * (jnp.log(1.0 + c) - jnp.log(1.0 - c))
        value[:, pl.ds(pl.multiple_of(q * piece, piece), piece)] = z.astype(value.dtype)
        copy(q).start()
        return carry

    def done(q, carry):
        copy(q).wait()
        return carry

    lax.fori_loop(0, pieces, one, 0, unroll=2)
    lax.fori_loop(0, pieces, done, 0)


def body(series, tap_values, tap_count, kept_frames, band_start):
    n_row, n_col = lax.axis_size("row"), lax.axis_size("col")
    n = n_row * n_col
    low = max(k for k in range(1, n_row + 1) if n_row % k == 0 and k * k <= n_row)
    block, grays = series.shape
    width = grays // n
    wide = -(-width // 256) * 256
    reach = tap_values.shape[0] // 2
    frames = n * block
    high = n_row // low
    sites = (2 + low) + (high - 1) * 2 * (1 + low) + 2 * high * low
    pieces = min(n, B // LANES)
    piece = B // pieces
    chunk = min(piece, 256)
    tiles = frames // TILE
    anywhere = pl.BlockSpec(memory_space=pltpu.HBM)
    vmem = pl.BlockSpec(memory_space=pltpu.VMEM)
    f32, i32, bf16 = jnp.float32, jnp.int32, jnp.bfloat16
    own, stage, weights = pl.pallas_call(
        functools.partial(prepare, (n, width, reach)),
        out_shape=[
            jax.ShapeDtypeStruct((pieces, block, piece), f32),
            jax.ShapeDtypeStruct((n, block, wide), f32),
            jax.ShapeDtypeStruct((tiles, TILE, TILE + 2 * reach), f32),
        ],
        in_specs=[anywhere] * 5,
        out_specs=[vmem] * 3,
        scratch_shapes=[
            pltpu.VMEM(series.shape, f32),
            pltpu.SMEM(tap_values.shape, f32),
            pltpu.SMEM(tap_count.shape, i32),
            pltpu.SMEM(kept_frames.shape, i32),
            pltpu.SMEM(band_start.shape, i32),
            pltpu.SemaphoreType.DMA((5,)),
        ],
        compiler_params=pltpu.CompilerParams(vmem_limit_bytes=32 * 1024 * 1024),
    )(series, tap_values, tap_count, kept_frames, band_start)
    band, turned = pl.pallas_call(
        functools.partial(exchange, (n_row, n_col, low)),
        out_shape=[
            jax.ShapeDtypeStruct((pieces, frames, piece), bf16),
            jax.ShapeDtypeStruct((wide, frames), bf16),
        ],
        in_specs=[vmem] * 3,
        out_specs=[vmem] * 2,
        scratch_shapes=[
            pltpu.VMEM((n + 2, block, piece), f32),
            pltpu.VMEM((n + 2, block, wide), f32),
            pltpu.VMEM((frames, chunk), f32),
            pltpu.SemaphoreType.DMA((n,)),
            pltpu.SemaphoreType.DMA((n,)),
            pltpu.SemaphoreType.DMA((n,)),
            pltpu.SemaphoreType.DMA((n,)),
            pltpu.SemaphoreType.DMA((sites,)),
            pltpu.SemaphoreType.DMA((n,)),
        ],
        compiler_params=pltpu.CompilerParams(
            collective_id=0, has_side_effects=True, vmem_limit_bytes=40 * 1024 * 1024
        ),
    )(own, stage, weights)
    out = pl.pallas_call(
        fisher,
        out_shape=jax.ShapeDtypeStruct((width, B), bf16),
        in_specs=[vmem] * 2,
        out_specs=anywhere,
        scratch_shapes=[
            pltpu.VMEM((width, B), bf16),
            pltpu.SemaphoreType.DMA((pieces,)),
        ],
        compiler_params=pltpu.CompilerParams(vmem_limit_bytes=32 * 1024 * 1024),
    )(turned, band)
    return out.T


def solution(mesh):
    placed = (P(("subj", "row", "col"), None), P(), P(), P("subj"), P("subj"))
    return jax.shard_map(
        body, mesh=mesh, in_specs=placed, out_specs=P("subj", ("row", "col")), check_vma=False
    )
```
